128 devices in a mesh: blk: 16 (over x, z_hi, core), act: 8 (over z_lo, y).
Axes of the slice: x: 4, y: 4, z: 4 (z_hi: 2, z_lo: 2; z = z_hi * 2 + z_lo), core: 2. Of those that a mesh axis runs over, the one named last changes fastest.
Arguments:
- field_pos: float32 [3, 98304], P(None, 'blk'), may hold values from -6 to 6
- field_vel: float32 [3, 98304], P(None, 'blk'), may hold values from -3 to 3
- field_acc: float32 [3, 98304], P(None, 'blk'), may hold values from -6 to 6
- field_jerk: float32 [3, 98304], P(None, 'blk'), may hold values from -6 to 6
- field_mass: float32 [98304], P('blk')
- levels: int32 [98304], P('blk'), may hold values from 0 to 3
- active_index: int32 [16, 8, 64], P('blk', 'act'), may hold values from 0 to 6143, as said below
- active_count: int32 [16, 8], P('blk', 'act'), may hold values from 1 to 64, 256 in all within a row
Outputs:
- updated: float32 [12, 16, 8, 64], P(None, 'blk', 'act')
The draws below stay inside these ranges and needn't reach their ends.
Inputs may be any that keep to these rules, and one draw needn't show every extreme that they name: `active_index`: within one block b the 8 lists hold distinct stars, live slots and dead ones alike. `active_count`: in every block b the counts sum to exactly 256, and one device of each block has all 64 slots live.
All inputs are finite; a program needn't handle non-finite values.
Results may differ from the reference program's by a relative error of at most 0.0003.
Values sent between devices are 32-bit elements; how exact they have to be, the bound alone decides.
No kernel may reach another device: no remote copies, remote signals or barrier semaphores. Data moves between devices by JAX's collectives and lax.ppermute only.
A program may use at most 64 MiB of HBM per device.

```python
import math
import jax
import jax.numpy as jnp
import numpy as np
from jax import lax

FIELD_DEV = 6144
BAL = 32
CAP = 64
N_FIELD = 98304
N_BLK = 16
N_ACT = 8


def draw_field_mass(key, part):
    key = jax.random.fold_in(key, 1)
    uniform_val = jax.random.uniform(key, (N_FIELD,), jnp.float32)
    masses = jnp.exp(jnp.log(10.0) * uniform_val)
    return (masses / (4.0 * N_FIELD)).astype(jnp.float32)


def draw_active_index(key, part):
    key = jax.random.fold_in(key, 2)
    row_keys = jax.random.split(key, N_BLK)
    orders = jax.vmap(lambda row_key: jax.random.permutation(row_key, FIELD_DEV))(row_keys)
    return orders[:, :N_ACT * CAP].reshape(N_BLK, N_ACT, CAP).astype(jnp.int32)


def plant(values, stream_key, low, largest):
    longest = values.shape.index(max(values.shape))
    spots = []
    for shift in (0, 1):
        where = [jax.random.randint(jax.random.fold_in(stream_key, axis), (), 0, length) for axis, length in enumerate(values.shape)]
        where[longest] = (where[longest] + shift) % values.shape[longest]
        spots.append(tuple(where))
    return values.at[spots[0]].set(low).at[spots[1]].set(largest)


def block_scale(key, extent, cuts, least, top_value):
    loudness, own = 1.0, jax.random.fold_in(key, 6)
    for axis_at, blocks in cuts:
        steps = jnp.exp(jax.random.uniform(jax.random.fold_in(own, axis_at), (blocks,), jnp.float32, least / len(cuts), top_value / len(cuts)))
        loudness = loudness * jnp.repeat(steps, extent[axis_at] // blocks).reshape([-1 if axis == axis_at else 1 for axis in range(len(extent))])
    return loudness


def split_up(count, total, limit, lean):
    portions = [(1 << 20) // math.isqrt(rank ** lean) + 1 for rank in range(2, count + 1)]
    surplus, holding = total - limit - (count - 1), [1] * (count - 1)
    while surplus > 0:
        candidates = [i for i in range(count - 1) if holding[i] < limit]
        pool, remaining = sum([portions[i] for i in candidates]), surplus
        for i in candidates:
            more = min(limit - holding[i], max(1, remaining * portions[i] // pool), surplus)
            holding[i] = holding[i] + more
            surplus = surplus - more
    return np.array([limit] + holding)


def uneven(key, number_of, total, limit, lean):
    if number_of == 2:
        one = jax.random.randint(key, (), max(1, total - limit), min(limit, total - 1) + 1)
        return jnp.stack([one, total - one])
    tallies = jnp.asarray(split_up(number_of, total, limit, lean), jnp.int32)
    couples = (number_of - 1) // 2
    giver, sink = tallies[1:1 + 2 * couples:2], tallies[2:2 + 2 * couples:2]
    margin = jnp.minimum(giver - 1, limit - sink)
    moved = jax.random.randint(jax.random.fold_in(key, 1), (couples,), 0, 1 << 20) % (margin + 1)
    tallies = tallies.at[1:1 + 2 * couples:2].set(giver - moved).at[2:2 + 2 * couples:2].set(sink + moved)
    return tallies[jax.random.permutation(jax.random.fold_in(key, 2), number_of)]


def scatter_about(stream_key, extent, scale, limit, cuts=(), kind=jnp.bfloat16):
    drawn = scale * jax.random.normal(stream_key, extent, jnp.float32)
    if cuts:
        drawn = drawn * block_scale(stream_key, extent, cuts, -0.22, 0.18)
    return jnp.clip(drawn, -limit, limit).astype(kind)


def setup_inputs(seed: int = 0) -> dict:
    arg_keys = jax.random.split(jax.random.key(seed), 9)
    field_pos = scatter_about(arg_keys[0], (3, N_FIELD), 1.0, 6.0, ((1, 16),), jnp.float32)
    field_vel = scatter_about(arg_keys[1], (3, N_FIELD), 0.5, 3.0, ((1, 16),), jnp.float32)
    field_acc = scatter_about(arg_keys[2], (3, N_FIELD), 1.0, 6.0, ((1, 16),), jnp.float32)
    field_jerk = scatter_about(arg_keys[3], (3, N_FIELD), 1.0, 6.0, ((1, 16),), jnp.float32)
    field_mass = draw_field_mass(jax.random.fold_in(arg_keys[8], 71), 0)
    levels = plant(jax.random.randint(arg_keys[5], (N_FIELD,), 0, 4), jax.random.fold_in(arg_keys[5], 1), 0, 3).astype(jnp.int32)
    active_index = draw_active_index(jax.random.fold_in(arg_keys[8], 71), 0)
    active_count = jax.vmap(lambda own: uneven(own, N_ACT, BAL * N_ACT, CAP, 2))(jax.random.split(arg_keys[7], N_BLK)).reshape((N_BLK, N_ACT)).astype(jnp.int32)
    return dict(field_pos=field_pos, field_vel=field_vel, field_acc=field_acc, field_jerk=field_jerk, field_mass=field_mass, levels=levels, active_index=active_index, active_count=active_count)


soften_sq = 0.01
now_ticks = 11
tick_length = 0.0625

def predict(pos, vel, acc, jerk, levels):
    period = jnp.left_shift(jnp.ones_like(levels), 4 - levels)
    elapse = jnp.remainder(jnp.full_like(levels, now_ticks), period).astype(jnp.float32) * tick_length
    pred_pos = pos + elapse * (vel + elapse * (acc / 2.0 + elapse * jerk / 6.0))
    pred_vel = vel + elapse * (acc + elapse * jerk / 2.0)
    return (pred_pos, pred_vel, elapse)

def pair_terms(act_pos, act_vel, src_pos, src_vel, src_mass):
    offset = src_pos[:, None, :] - act_pos[:, :, None]
    relvel = src_vel[:, None, :] - act_vel[:, :, None]
    dist_sq = lax.optimization_barrier(jnp.sum(offset * offset, axis=0)) + soften_sq
    inverse = lax.rsqrt(dist_sq)
    inv_sq = inverse * inverse
    strength = src_mass[None, :] * inverse * inv_sq
    radial = 3.0 * lax.optimization_barrier(jnp.sum(offset * relvel, axis=0)) * inv_sq
    new_acc = lax.optimization_barrier(jnp.sum(strength * offset, axis=-1))
    new_jerk = lax.optimization_barrier(jnp.sum(strength * (relvel - radial * offset), axis=-1))
    return (new_acc, new_jerk)

def correct(pred_pos, pred_vel, old_acc, old_jerk, new_acc, new_jerk, elapse):
    span = elapse[None, :]
    change = old_acc - new_acc
    snap_term = (-6.0 * change - span * (4.0 * old_jerk + 2.0 * new_jerk)) / (span * span)
    crackle = (12.0 * change + 6.0 * span * (old_jerk + new_jerk)) / (span * span * span)
    span_four = span * span * span * span
    new_pos = pred_pos + span_four / 24.0 * snap_term + span_four * span / 120.0 * crackle
    new_vel = pred_vel + span * span * span / 6.0 * snap_term + span_four / 24.0 * crackle
    return jnp.concatenate([new_pos, new_vel, new_acc, new_jerk], axis=0)

def reference(field_pos, field_vel, field_acc, field_jerk, field_mass, levels, active_index, active_count):
    pred_pos, pred_vel, elapse = predict(field_pos, field_vel, field_acc, field_jerk, levels)

    def one_row(block_id):
        global_ids = active_index[block_id].reshape(-1) + block_id * FIELD_DEV
        act_pos = pred_pos[:, global_ids]
        act_vel = pred_vel[:, global_ids]

        def sweep(sums, source_id):
            start = (source_id * FIELD_DEV).astype(jnp.int32)
            src_pos = lax.dynamic_slice_in_dim(pred_pos, start, FIELD_DEV, 1)
            src_vel = lax.dynamic_slice_in_dim(pred_vel, start, FIELD_DEV, 1)
            src_mass = lax.dynamic_slice_in_dim(field_mass, start, FIELD_DEV, 0)
            part_acc, part_jerk = pair_terms(act_pos, act_vel, src_pos, src_vel, src_mass)
            return ((sums[0] + part_acc, sums[1] + part_jerk), None)
        zeros = jnp.zeros_like(act_pos)
        (new_acc, new_jerk), _ = lax.scan(sweep, (zeros, zeros), jnp.arange(N_BLK, dtype=jnp.int32))
        result = correct(act_pos, act_vel, field_acc[:, global_ids], field_jerk[:, global_ids], new_acc, new_jerk, elapse[global_ids])
        slot_ids = jnp.arange(CAP, dtype=jnp.int32)
        live_slot = (slot_ids[None, :] < active_count[block_id][:, None]).reshape(-1)
        result = jnp.where(live_slot[None, :], result, jnp.zeros_like(result))
        return result.reshape(12, N_ACT, CAP)
    per_row = lax.map(one_row, jnp.arange(N_BLK, dtype=jnp.int32))
    return jnp.transpose(per_row, (1, 0, 2, 3))
```

```python
import functools

import jax
import jax.numpy as jnp
from jax import lax
from jax.experimental import pallas as pl
from jax.experimental.pallas import tpu as pltpu
from jax.sharding import PartitionSpec as P

F32 = jnp.float32
BF16 = jnp.bfloat16
SOFTEN = 0.01
NOW = 11
TICK = 0.0625
GRID = 16.0
LANES = 128
CAP = 64
STEP = 2048
VMEM = 44 << 20


def round_bf16(x):
    return x.astype(BF16).astype(F32)


def split2(x):
    a = round_bf16(x)
    return a, round_bf16(x - a)


def split3(x):
    a = round_bf16(x)
    b = round_bf16(x - a)
    return a, b, x - a - b


def coarse(x):
    c = round_bf16(jnp.round(x * GRID) * (1.0 / GRID))
    return c, x - c


def rows_sum(x):
    return jnp.sum(x, axis=0, keepdims=True)


def basis(p, v):
    c, d = coarse(p)
    e, f = coarse(v)
    parts = (c, *split2(d)), (e, *split2(f))
    norms = (
        rows_sum(c * c),
        rows_sum(2.0 * c * d + d * d),
        rows_sum(c * e),
        rows_sum(c * f + d * e + d * f),
    )
    return parts, norms


def select_kernel(
    idx_hbm, cnt_hbm, pos_hbm, vel_hbm, acc_hbm, jerk_hbm, mass_hbm, lev_hbm,
    send_ref, own_ref, pv_ref, idx, cnt, pos, vel, acc, jerk, mass, lev, table, sem,
):
    pairs = (
        (lev_hbm, lev), (pos_hbm, pos), (vel_hbm, vel), (acc_hbm, acc), (jerk_hbm, jerk), (mass_hbm, mass),
        (idx_hbm, idx), (cnt_hbm, cnt),
    )
    copies = [pltpu.make_async_copy(a, b, sem.at[k]) for k, (a, b) in enumerate(pairs)]
    for copy in copies:
        copy.start()
    for copy in copies:
        copy.wait()
    level = lev[...]
    period = jnp.left_shift(jnp.ones_like(level), 4 - level)
    e = lax.rem(jnp.full_like(level, NOW), period).astype(F32) * TICK
    x, u, a, j = pos[...], vel[...], acc[...], jerk[...]
    p = x + e * (u + e * (a * 0.5 + e * j / 6.0))
    v = u + e * (a + e * j * 0.5)
    pv_ref[0:3, :] = p
    pv_ref[3:6, :] = v
    pv_ref[6:7, :] = mass[...]
    table[0:3, :] = p
    table[3:6, :] = v
    table[6:9, :] = a
    table[9:12, :] = j
    table[12:13, :] = e
    lane = lax.broadcasted_iota(jnp.int32, (16, LANES), 1)
    got = jnp.zeros((16, LANES), F32)
    for s in range(CAP):
        i = idx[0, 0, s]
        block = table[:, pl.ds(pl.multiple_of((i >> 7) * LANES, LANES), LANES)]
        got = jnp.where(lane == s, pltpu.roll(block, (s - i) & (LANES - 1), 1), got)
    count = cnt[0, 0]
    own_ref[0:13, :] = got[0:13]
    own_ref[13:16, :] = jnp.full((3, LANES), count.astype(F32))
    row = lax.broadcasted_iota(jnp.int32, (8, LANES), 0)
    live = lax.broadcasted_iota(jnp.int32, (8, LANES), 1) < count
    out = jnp.where(row < 6, jnp.where(live, got[0:8], 0.0), jnp.where(row == 6, count.astype(F32), 0.0))
    for k in range(send_ref.shape[0]):
        send_ref[k] = out


def prepare_kernel(pv_ref, ys_ref, mt_ref, b_ref, m_ref):
    n = pv_ref.shape[1]
    p, v, m = pv_ref[0:3, :], pv_ref[3:6, :], pv_ref[6:7, :]
    (pp, vv), norms = basis(p, v)
    for k, x in enumerate((*pp, *vv)):
        b_ref[3 * k : 3 * k + 3, :] = x
    b_ref[18:20, :] = jnp.ones((2, n), F32)
    for k, x in enumerate(norms):
        for t, y in enumerate(split3(x)):
            b_ref[20 + 3 * k + t : 21 + 3 * k + t, :] = y
    m_ref[...] = jnp.zeros(m_ref.shape, F32)
    for k, x in enumerate((m * p, m * v)):
        for t, y in enumerate(split3(x)):
            m_ref[8 * t + 3 * k : 8 * t + 3 * k + 3, :] = y
    for t, y in enumerate(split3(m)):
        m_ref[8 * t + 6 : 8 * t + 7, :] = y
    mt_ref[...] = m_ref[...].astype(BF16)

    def body(i, _):
        o = pl.multiple_of(i * LANES, LANES)
        x = b_ref[:, pl.ds(o, LANES)].astype(BF16)
        ys_ref[pl.ds(o, LANES), :] = jnp.concatenate([x, x, x, x], axis=0).T
        return 0

    lax.fori_loop(0, n // LANES, body, 0, unroll=4)


def fill_weights(p, v, wq_ref, wr_ref):
    n = p.shape[1]
    (pp, vv), (cc, dn, ce, gn) = basis(p, v)
    wq_ref[...] = jnp.zeros(wq_ref.shape, F32)
    wr_ref[...] = jnp.zeros(wr_ref.shape, F32)
    cc, dn, ce, gn = split3(cc), split3(dn + SOFTEN), split3(ce), split3(gn)
    for w in range(3):
        o = 32 * w
        for k in range(3):
            wq_ref[o + 3 * k : o + 3 * k + 3, :] = -2.0 * pp[w]
            wr_ref[o + 3 * k : o + 3 * k + 3, :] = -vv[w]
            wr_ref[o + 9 + 3 * k : o + 12 + 3 * k, :] = -pp[w]
        wq_ref[o + 18 : o + 19, :] = cc[w]
        wq_ref[o + 19 : o + 20, :] = dn[w]
        wr_ref[o + 18 : o + 19, :] = ce[w]
        wr_ref[o + 19 : o + 20, :] = gn[w]
    wq_ref[20:26, :] = jnp.ones((6, n), F32)
    wr_ref[26:32, :] = jnp.ones((6, n), F32)


def sweep_kernel(recv_ref, ys_ref, mt_ref, out_ref, act_ref, res_ref, wq_ref, wr_ref, wqb_ref, wrb_ref):
    lists = recv_ref.shape[0]
    stars = ys_ref.shape[0]
    lane = lax.broadcasted_iota(jnp.int32, (8, LANES), 1)
    act_ref[...] = jnp.zeros(act_ref.shape, F32)
    offsets = []
    total = jnp.int32(0)
    for k in range(lists):
        x = recv_ref[k]
        offsets.append(total)
        shift = total & (LANES - 1)
        o = pl.multiple_of((total >> 7) * LANES, LANES)
        x = pltpu.roll(x, shift, 1)
        act_ref[:, pl.ds(o, LANES)] += jnp.where(lane >= shift, x, 0.0)
        act_ref[:, pl.ds(o + LANES, LANES)] += jnp.where(lane < shift, x, 0.0)
        total = total + jnp.max(recv_ref[k, 6:7, :].astype(jnp.int32))
    size = wq_ref.shape[1]
    fill_weights(act_ref[0:3, 0:size], act_ref[3:6, 0:size], wq_ref, wr_ref)
    wqb_ref[...] = wq_ref[...].astype(BF16)
    wrb_ref[...] = wr_ref[...].astype(BF16)

    def tile(a, width):
        cols = pl.ds(a, width)
        w = jnp.concatenate([wqb_ref[:, cols], wrb_ref[:, cols]], axis=1)

        def body(i, carry):
            high, low = carry
            o = pl.multiple_of(i * STEP, STEP)
            qr = jnp.dot(ys_ref[pl.ds(o, STEP), :], w, preferred_element_type=F32)
            q, rw = qr[:, :width], qr[:, width:]
            inv = lax.rsqrt(q)
            inv2 = inv * inv
            s = inv * inv2
            st = jnp.concatenate([s, s * inv2 * rw], axis=1)
            hi = st.astype(BF16)
            lo = (st - hi.astype(F32)).astype(BF16)
            high = high + jnp.dot(mt_ref[:, pl.ds(o, STEP)], hi, preferred_element_type=F32)
            low = low + jnp.dot(mt_ref[0:16, pl.ds(o, STEP)], lo, preferred_element_type=F32)
            return high, low

        zero = jnp.zeros((32, 2 * width), F32), jnp.zeros((16, 2 * width), F32)
        high, low = lax.fori_loop(0, stars // STEP, body, zero)
        x = (high[16:24] + low[8:16]) + (high[8:16] + low[0:8]) + high[0:8]
        s, t = x[:, :width], x[:, width:]
        p, v = act_ref[0:3, cols], act_ref[3:6, cols]
        res_ref[0:3, cols] = s[0:3] - p * s[6:7]
        res_ref[3:6, cols] = s[3:6] - v * s[6:7] - 3.0 * (t[0:3] - p * t[6:7])

    tiles = (total + (LANES - 1)) >> 7
    pairs = tiles >> 1

    def two(t, _):
        tile(pl.multiple_of(t * 2 * LANES, LANES), 2 * LANES)
        return 0

    def one(t, _):
        tile(pl.multiple_of(t * LANES, LANES), LANES)
        return 0

    lax.fori_loop(0, pairs, two, 0)
    lax.fori_loop(2 * pairs, tiles, one, 0)
    for k in range(lists):
        shift = offsets[k] & (LANES - 1)
        o = pl.multiple_of((offsets[k] >> 7) * LANES, LANES)
        back = (LANES - shift) & (LANES - 1)
        a = pltpu.roll(res_ref[:, pl.ds(o, LANES)], back, 1)
        b = pltpu.roll(res_ref[:, pl.ds(o + LANES, LANES)], back, 1)
        out_ref[k] = jnp.where(lane < LANES - shift, a, b)


def finish_kernel(recv_ref, own_ref, out_ref):
    x = recv_ref[0]
    for k in range(1, recv_ref.shape[0]):
        x = x + recv_ref[k]
    new_acc, new_jerk = x[0:3, :CAP], x[3:6, :CAP]
    own = own_ref[:, :CAP]
    p, v, acc, jerk, e = own[0:3], own[3:6], own[6:9], own[9:12], own[12:13]
    change = acc - new_acc
    e2 = e * e
    e3 = e2 * e
    e4 = e2 * e2
    snap = (-6.0 * change - e * (4.0 * jerk + 2.0 * new_jerk)) / e2
    crackle = (12.0 * change + 6.0 * e * (jerk + new_jerk)) / e3
    pos = p + e4 / 24.0 * snap + e4 * e / 120.0 * crackle
    vel = v + e3 / 6.0 * snap + e4 / 24.0 * crackle
    live = lax.broadcasted_iota(jnp.int32, (3, CAP), 1).astype(F32) < own[13:14]
    for k, y in enumerate((pos, vel, new_acc, new_jerk)):
        y = jnp.where(live, y, 0.0)
        for c in range(3):
            out_ref[3 * k + c, 0] = y[c : c + 1]


def spec(space):
    return pl.BlockSpec(memory_space=space)


def params(limit=VMEM):
    return pltpu.CompilerParams(vmem_limit_bytes=limit)


def on_device(groups, field_pos, field_vel, field_acc, field_jerk, field_mass, levels, active_index, active_count):
    n = field_pos.shape[1]
    lists = len(groups[0])
    vmem = spec(pltpu.VMEM)
    send, own, pv = pl.pallas_call(
        select_kernel,
        out_shape=(
            jax.ShapeDtypeStruct((lists, 8, LANES), F32),
            jax.ShapeDtypeStruct((16, LANES), F32),
            jax.ShapeDtypeStruct((8, n), F32),
        ),
        in_specs=[spec(pltpu.HBM)] * 8,
        scratch_shapes=[pltpu.SMEM((1, 1, CAP), jnp.int32), pltpu.SMEM((1, 1), jnp.int32)]
        + [pltpu.VMEM((3, n), F32)] * 4
        + [pltpu.VMEM((1, n), F32), pltpu.VMEM((1, n), jnp.int32), pltpu.VMEM((16, n), F32)]
        + [pltpu.SemaphoreType.DMA((8,))],
        compiler_params=params(60 << 20),
        cost_estimate=pl.CostEstimate(flops=1 << 20, bytes_accessed=1 << 20, transcendentals=0),
        name="select",
    )(
        active_index, active_count, field_pos, field_vel, field_acc, field_jerk,
        field_mass.reshape(1, n), levels.reshape(1, n),
    )
    axes = ("blk", "act")
    recv = lax.all_to_all(send, axes, 0, 0, axis_index_groups=groups, tiled=True)
    ys, mt = pl.pallas_call(
        prepare_kernel,
        out_shape=(jax.ShapeDtypeStruct((n, LANES), BF16), jax.ShapeDtypeStruct((32, n), BF16)),
        in_specs=[vmem],
        scratch_shapes=[pltpu.VMEM((32, n), F32)] * 2,
        compiler_params=params(),
        cost_estimate=pl.CostEstimate(flops=1 << 22, bytes_accessed=4 << 20, transcendentals=0),
        name="prepare",
    )(pv)
    size = lists * CAP
    part = pl.pallas_call(
        sweep_kernel,
        out_shape=jax.ShapeDtypeStruct((lists, 8, LANES), F32),
        in_specs=[vmem] * 3,
        scratch_shapes=[pltpu.VMEM((8, size + LANES), F32)] * 2
        + [pltpu.VMEM((LANES, size), F32)] * 2
        + [pltpu.VMEM((LANES, size), BF16)] * 2,
        compiler_params=params(),
        cost_estimate=pl.CostEstimate(flops=10 << 30, bytes_accessed=4 << 20, transcendentals=0),
        name="sweep",
    )(recv, ys, mt)
    back = lax.all_to_all(part, axes, 0, 0, axis_index_groups=groups, tiled=True)
    out = pl.pallas_call(
        finish_kernel,
        out_shape=jax.ShapeDtypeStruct((12, 1, 1, CAP), F32),
        in_specs=[vmem, vmem],
        compiler_params=params(),
        name="finish",
    )(back, own)
    return out


def list_groups():
    groups = []
    for y in range(4):
        for flip in range(2):
            group = []
            for b in range(16):
                z_hi = (b >> 1) & 1
                z_lo = z_hi ^ flip
                group.append(b * 8 + z_lo * 4 + y)
            groups.append(group)
    return groups


def solution(mesh):
    return jax.shard_map(
        functools.partial(on_device, list_groups()),
        mesh=mesh,
        in_specs=(
            P(None, "blk"),
            P(None, "blk"),
            P(None, "blk"),
            P(None, "blk"),
            P("blk"),
            P("blk"),
            P("blk", "act", None),
            P("blk", "act"),
        ),
        out_specs=P(None, "blk", "act", None),
        check_vma=False,
    )
```

```python
import functools

import jax
import jax.numpy as jnp
from jax import lax
from jax.experimental import pallas as pl
from jax.experimental.pallas import tpu as pltpu
from jax.sharding import PartitionSpec as P

F32 = jnp.float32
BF16 = jnp.bfloat16
SOFTEN = 0.01
NOW = 11
TICK = 0.0625
GRID = 16.0
LANES = 128
CAP = 64
VMEM = 44 << 20


def round_bf16(x):
    return x.astype(BF16).astype(F32)


def split2(x):
    a = round_bf16(x)
    return a, round_bf16(x - a)


def split3(x):
    a = round_bf16(x)
    b = round_bf16(x - a)
    return a, b, x - a - b


def coarse(x):
    c = round_bf16(jnp.round(x * GRID) * (1.0 / GRID))
    return c, x - c


def rows_sum(x):
    return jnp.sum(x, axis=0, keepdims=True)


def basis(p, v):
    c, d = coarse(p)
    e, f = coarse(v)
    parts = (c, *split2(d)), (e, *split2(f))
    norms = (
        rows_sum(c * c),
        rows_sum(2.0 * c * d + d * d),
        rows_sum(c * e),
        rows_sum(c * f + d * e + d * f),
    )
    return parts, norms


def select_kernel(
    idx_hbm, cnt_hbm, pos_hbm, vel_hbm, acc_hbm, jerk_hbm, mass_hbm, lev_hbm,
    send_ref, own_ref, pv_ref, idx, cnt, pos, vel, acc, jerk, mass, lev, table, sem,
):
    pairs = (
        (lev_hbm, lev), (pos_hbm, pos), (vel_hbm, vel), (acc_hbm, acc), (jerk_hbm, jerk), (mass_hbm, mass),
        (idx_hbm, idx), (cnt_hbm, cnt),
    )
    copies = [pltpu.make_async_copy(a, b, sem.at[k]) for k, (a, b) in enumerate(pairs)]
    for copy in copies:
        copy.start()
    for copy in copies:
        copy.wait()
    level = lev[...]
    period = jnp.left_shift(jnp.ones_like(level), 4 - level)
    e = lax.rem(jnp.full_like(level, NOW), period).astype(F32) * TICK
    x, u, a, j = pos[...], vel[...], acc[...], jerk[...]
    p = x + e * (u + e * (a * 0.5 + e * j / 6.0))
    v = u + e * (a + e * j * 0.5)
    pv_ref[0:3, :] = p
    pv_ref[3:6, :] = v
    pv_ref[6:7, :] = mass[...]
    table[0:3, :] = p
    table[3:6, :] = v
    table[6:9, :] = a
    table[9:12, :] = j
    table[12:13, :] = e
    lane = lax.broadcasted_iota(jnp.int32, (16, LANES), 1)
    got = jnp.zeros((16, LANES), F32)
    for s in range(CAP):
        i = idx[0, 0, s]
        block = table[:, pl.ds(pl.multiple_of((i >> 7) * LANES, LANES), LANES)]
        got = jnp.where(lane == s, pltpu.roll(block, (s - i) & (LANES - 1), 1), got)
    count = cnt[0, 0]
    own_ref[0:13, :] = got[0:13]
    own_ref[13:16, :] = jnp.full((3, LANES), count.astype(F32))
    row = lax.broadcasted_iota(jnp.int32, (8, LANES), 0)
    live = lax.broadcasted_iota(jnp.int32, (8, LANES), 1) < count
    out = jnp.where(row < 6, jnp.where(live, got[0:8], 0.0), jnp.where(row == 6, count.astype(F32), 0.0))
    for k in range(send_ref.shape[0]):
        send_ref[k] = out


def prepare_kernel(pv_ref, ys_ref, mt_ref, b_ref, m_ref):
    n = pv_ref.shape[1]
    p, v, m = pv_ref[0:3, :], pv_ref[3:6, :], pv_ref[6:7, :]
    (pp, vv), norms = basis(p, v)
    for k, x in enumerate((*pp, *vv)):
        b_ref[3 * k : 3 * k + 3, :] = x
    b_ref[18:20, :] = jnp.ones((2, n), F32)
    for k, x in enumerate(norms):
        for t, y in enumerate(split3(x)):
            b_ref[20 + 3 * k + t : 21 + 3 * k + t, :] = y
    m_ref[...] = jnp.zeros(m_ref.shape, F32)
    for k, x in enumerate((m * p, m * v)):
        for t, y in enumerate(split3(x)):
            m_ref[8 * t + 3 * k : 8 * t + 3 * k + 3, :] = y
    for t, y in enumerate(split3(m)):
        m_ref[8 * t + 6 : 8 * t + 7, :] = y
    mt_ref[...] = m_ref[...].astype(BF16)

    def body(i, _):
        o = pl.multiple_of(i * LANES, LANES)
        x = b_ref[:, pl.ds(o, LANES)].astype(BF16)
        ys_ref[pl.ds(o, LANES), :] = jnp.concatenate([x, x, x, x], axis=0).T
        return 0

    lax.fori_loop(0, n // LANES, body, 0, unroll=4)


def fill_weights(p, v, wq_ref, wr_ref):
    n = p.shape[1]
    (pp, vv), (cc, dn, ce, gn) = basis(p, v)
    wq_ref[...] = jnp.zeros(wq_ref.shape, F32)
    wr_ref[...] = jnp.zeros(wr_ref.shape, F32)
    cc, dn, ce, gn = split3(cc), split3(dn + SOFTEN), split3(ce), split3(gn)
    for w in range(3):
        o = 32 * w
        for k in range(3):
            wq_ref[o + 3 * k : o + 3 * k + 3, :] = -2.0 * pp[w]
            wr_ref[o + 3 * k : o + 3 * k + 3, :] = -vv[w]
            wr_ref[o + 9 + 3 * k : o + 12 + 3 * k, :] = -pp[w]
        wq_ref[o + 18 : o + 19, :] = cc[w]
        wq_ref[o + 19 : o + 20, :] = dn[w]
        wr_ref[o + 18 : o + 19, :] = ce[w]
        wr_ref[o + 19 : o + 20, :] = gn[w]
    wq_ref[20:26, :] = jnp.ones((6, n), F32)
    wr_ref[26:32, :] = jnp.ones((6, n), F32)


def sweep_kernel(recv_ref, ys_ref, mt_ref, out_ref, act_ref, res_ref, wq_ref, wr_ref, wa_ref, wb_ref):
    lists = recv_ref.shape[0]
    stars = ys_ref.shape[0]
    lane = lax.broadcasted_iota(jnp.int32, (8, LANES), 1)
    act_ref[...] = jnp.zeros(act_ref.shape, F32)
    offsets = []
    total = jnp.int32(0)
    for k in range(lists):
        x = recv_ref[k]
        offsets.append(total)
        shift = total & (LANES - 1)
        o = pl.multiple_of((total >> 7) * LANES, LANES)
        x = pltpu.roll(x, shift, 1)
        act_ref[:, pl.ds(o, LANES)] += jnp.where(lane >= shift, x, 0.0)
        act_ref[:, pl.ds(o + LANES, LANES)] += jnp.where(lane < shift, x, 0.0)
        total = total + jnp.max(recv_ref[k, 6:7, :].astype(jnp.int32))
    size = wq_ref.shape[1]
    fill_weights(act_ref[0:3, 0:size], act_ref[3:6, 0:size], wq_ref, wr_ref)
    for w in (wa_ref, wb_ref):
        w[0] = wq_ref[...].astype(BF16)
        w[1] = wr_ref[...].astype(BF16)

    def dot(a, b):
        return jnp.dot(a, b, preferred_element_type=F32)

    def tile(t, _):
        cols = pl.ds(pl.multiple_of(t * LANES, LANES), LANES)
        half = stars // 2
        parts = []
        for h, w in enumerate((wa_ref, wb_ref)):
            rows = slice(h * half, (h + 1) * half)
            qr = dot(ys_ref[rows, :], jnp.concatenate([w[0, :, cols], w[1, :, cols]], axis=1))
            q, rw = qr[:, :LANES], qr[:, LANES:]
            inv = lax.rsqrt(q)
            inv2 = inv * inv
            s = inv * inv2
            st = jnp.concatenate([s, s * inv2 * rw], axis=1)
            hi = st.astype(BF16)
            lo = (st - hi.astype(F32)).astype(BF16)
            parts.append((dot(mt_ref[:, rows], hi), dot(mt_ref[0:16, rows], lo)))
        high = parts[0][0] + parts[1][0]
        low = parts[0][1] + parts[1][1]
        x = (high[16:24] + low[8:16]) + (high[8:16] + low[0:8]) + high[0:8]
        s, t = x[:, :LANES], x[:, LANES:]
        p, v = act_ref[0:3, cols], act_ref[3:6, cols]
        res_ref[0:3, cols] = s[0:3] - p * s[6:7]
        res_ref[3:6, cols] = s[3:6] - v * s[6:7] - 3.0 * (t[0:3] - p * t[6:7])
        return 0

    lax.fori_loop(0, (total + (LANES - 1)) >> 7, tile, 0)
    for k in range(lists):
        shift = offsets[k] & (LANES - 1)
        o = pl.multiple_of((offsets[k] >> 7) * LANES, LANES)
        back = (LANES - shift) & (LANES - 1)
        a = pltpu.roll(res_ref[:, pl.ds(o, LANES)], back, 1)
        b = pltpu.roll(res_ref[:, pl.ds(o + LANES, LANES)], back, 1)
        out_ref[k] = jnp.where(lane < LANES - shift, a, b)


def finish_kernel(recv_ref, own_ref, out_ref):
    x = recv_ref[0]
    for k in range(1, recv_ref.shape[0]):
        x = x + recv_ref[k]
    new_acc, new_jerk = x[0:3, :CAP], x[3:6, :CAP]
    own = own_ref[:, :CAP]
    p, v, acc, jerk, e = own[0:3], own[3:6], own[6:9], own[9:12], own[12:13]
    change = acc - new_acc
    e2 = e * e
    e3 = e2 * e
    e4 = e2 * e2
    snap = (-6.0 * change - e * (4.0 * jerk + 2.0 * new_jerk)) / e2
    crackle = (12.0 * change + 6.0 * e * (jerk + new_jerk)) / e3
    pos = p + e4 / 24.0 * snap + e4 * e / 120.0 * crackle
    vel = v + e3 / 6.0 * snap + e4 / 24.0 * crackle
    live = lax.broadcasted_iota(jnp.int32, (3, CAP), 1).astype(F32) < own[13:14]
    for k, y in enumerate((pos, vel, new_acc, new_jerk)):
        y = jnp.where(live, y, 0.0)
        for c in range(3):
            out_ref[3 * k + c, 0] = y[c : c + 1]


def spec(space):
    return pl.BlockSpec(memory_space=space)


def params(limit=VMEM):
    return pltpu.CompilerParams(vmem_limit_bytes=limit)


def on_device(groups, field_pos, field_vel, field_acc, field_jerk, field_mass, levels, active_index, active_count):
    n = field_pos.shape[1]
    lists = len(groups[0])
    vmem = spec(pltpu.VMEM)
    send, own, pv = pl.pallas_call(
        select_kernel,
        out_shape=(
            jax.ShapeDtypeStruct((lists, 8, LANES), F32),
            jax.ShapeDtypeStruct((16, LANES), F32),
            jax.ShapeDtypeStruct((8, n), F32),
        ),
        in_specs=[spec(pltpu.HBM)] * 8,
        scratch_shapes=[pltpu.SMEM((1, 1, CAP), jnp.int32), pltpu.SMEM((1, 1), jnp.int32)]
        + [pltpu.VMEM((3, n), F32)] * 4
        + [pltpu.VMEM((1, n), F32), pltpu.VMEM((1, n), jnp.int32), pltpu.VMEM((16, n), F32)]
        + [pltpu.SemaphoreType.DMA((8,))],
        compiler_params=params(60 << 20),
        cost_estimate=pl.CostEstimate(flops=1 << 20, bytes_accessed=1 << 20, transcendentals=0),
        name="select",
    )(
        active_index, active_count, field_pos, field_vel, field_acc, field_jerk,
        field_mass.reshape(1, n), levels.reshape(1, n),
    )
    axes = ("blk", "act")
    recv = lax.all_to_all(send, axes, 0, 0, axis_index_groups=groups, tiled=True)
    ys, mt = pl.pallas_call(
        prepare_kernel,
        out_shape=(jax.ShapeDtypeStruct((n, LANES), BF16), jax.ShapeDtypeStruct((32, n), BF16)),
        in_specs=[vmem],
        scratch_shapes=[pltpu.VMEM((32, n), F32)] * 2,
        compiler_params=params(),
        cost_estimate=pl.CostEstimate(flops=1 << 22, bytes_accessed=4 << 20, transcendentals=0),
        name="prepare",
    )(pv)
    size = lists * CAP
    part = pl.pallas_call(
        sweep_kernel,
        out_shape=jax.ShapeDtypeStruct((lists, 8, LANES), F32),
        in_specs=[vmem] * 3,
        scratch_shapes=[pltpu.VMEM((8, size + LANES), F32)] * 2
        + [pltpu.VMEM((LANES, size), F32)] * 2
        + [pltpu.VMEM((2, LANES, size), BF16)] * 2,
        compiler_params=params(),
        cost_estimate=pl.CostEstimate(flops=10 << 30, bytes_accessed=4 << 20, transcendentals=0),
        name="sweep",
    )(recv, ys, mt)
    back = lax.all_to_all(part, axes, 0, 0, axis_index_groups=groups, tiled=True)
    out = pl.pallas_call(
        finish_kernel,
        out_shape=jax.ShapeDtypeStruct((12, 1, 1, CAP), F32),
        in_specs=[vmem, vmem],
        compiler_params=params(),
        name="finish",
    )(back, own)
    return out


def list_groups():
    groups = []
    for y in range(4):
        for flip in range(2):
            group = []
            for b in range(16):
                z_hi = (b >> 1) & 1
                z_lo = z_hi ^ flip
                group.append(b * 8 + z_lo * 4 + y)
            groups.append(group)
    return groups


def solution(mesh):
    return jax.shard_map(
        functools.partial(on_device, list_groups()),
        mesh=mesh,
        in_specs=(
            P(None, "blk"),
            P(None, "blk"),
            P(None, "blk"),
            P(None, "blk"),
            P("blk"),
            P("blk"),
            P("blk", "act", None),
            P("blk", "act"),
        ),
        out_specs=P(None, "blk", "act", None),
        check_vma=False,
    )
```

```python
import functools

import jax
import jax.numpy as jnp
from jax import lax
from jax.experimental import pallas as pl
from jax.experimental.pallas import tpu as pltpu
from jax.sharding import PartitionSpec as P

F32 = jnp.float32
BF16 = jnp.bfloat16
SOFTEN = 0.01
NOW = 11
TICK = 0.0625
GRID = 16.0
LANES = 128
CAP = 64
VMEM = 44 << 20


def round_bf16(x):
    return x.astype(BF16).astype(F32)


def split2(x):
    a = round_bf16(x)
    return a, round_bf16(x - a)


def split3(x):
    a = round_bf16(x)
    b = round_bf16(x - a)
    return a, b, x - a - b


def coarse(x):
    c = round_bf16(jnp.round(x * GRID) * (1.0 / GRID))
    return c, x - c


def rows_sum(x):
    return jnp.sum(x, axis=0, keepdims=True)


def basis(p, v):
    c, d = coarse(p)
    e, f = coarse(v)
    parts = (c, *split2(d)), (e, *split2(f))
    norms = (
        rows_sum(c * c),
        rows_sum(2.0 * c * d + d * d),
        rows_sum(c * e),
        rows_sum(c * f + d * e + d * f),
    )
    return parts, norms


def select_kernel(
    cnt_hbm, idx_hbm, pos_hbm, vel_hbm, acc_hbm, jerk_hbm, mass_hbm, lev_hbm,
    send_ref, own_ref, pv_ref, idx, cnt, pos, vel, acc, jerk, mass, lev, table, sem,
):
    pairs = (
        (lev_hbm, lev), (pos_hbm, pos), (vel_hbm, vel), (acc_hbm, acc), (jerk_hbm, jerk), (mass_hbm, mass),
        (idx_hbm, idx), (cnt_hbm, cnt),
    )
    copies = [pltpu.make_async_copy(a, b, sem.at[k]) for k, (a, b) in enumerate(pairs)]
    for copy in copies:
        copy.start()
    for copy in copies:
        copy.wait()
    level = lev[...]
    period = jnp.left_shift(jnp.ones_like(level), 4 - level)
    e = lax.rem(jnp.full_like(level, NOW), period).astype(F32) * TICK
    x, u, a, j = pos[...], vel[...], acc[...], jerk[...]
    p = x + e * (u + e * (a * 0.5 + e * j / 6.0))
    v = u + e * (a + e * j * 0.5)
    pv_ref[0:3, :] = p
    pv_ref[3:6, :] = v
    pv_ref[6:7, :] = mass[...]
    table[0:3, :] = p
    table[3:6, :] = v
    table[6:9, :] = a
    table[9:12, :] = j
    table[12:13, :] = e
    lane = lax.broadcasted_iota(jnp.int32, (16, LANES), 1)
    got = jnp.zeros((16, LANES), F32)
    for s in range(CAP):
        i = idx[0, 0, s]
        block = table[:, pl.ds(pl.multiple_of((i >> 7) * LANES, LANES), LANES)]
        got = jnp.where(lane == s, pltpu.roll(block, (s - i) & (LANES - 1), 1), got)
    count = cnt[0, 0]
    own_ref[0:13, :] = got[0:13]
    own_ref[13:16, :] = jnp.full((3, LANES), count.astype(F32))
    row = lax.broadcasted_iota(jnp.int32, (8, LANES), 0)
    live = lax.broadcasted_iota(jnp.int32, (8, LANES), 1) < count
    out = jnp.where(row < 6, jnp.where(live, got[0:8], 0.0), jnp.where(row == 6, count.astype(F32), 0.0))
    for k in range(send_ref.shape[0]):
        send_ref[k] = out


def prepare_kernel(pv_ref, ys_ref, mt_ref, b_ref, m_ref):
    n = pv_ref.shape[1]
    p, v, m = pv_ref[0:3, :], pv_ref[3:6, :], pv_ref[6:7, :]
    (pp, vv), norms = basis(p, v)
    for k, x in enumerate((*pp, *vv)):
        b_ref[3 * k : 3 * k + 3, :] = x
    b_ref[18:20, :] = jnp.ones((2, n), F32)
    for k, x in enumerate(norms):
        for t, y in enumerate(split3(x)):
            b_ref[20 + 3 * k + t : 21 + 3 * k + t, :] = y
    m_ref[...] = jnp.zeros(m_ref.shape, F32)
    for k, x in enumerate((m * p, m * v)):
        for t, y in enumerate(split3(x)):
            m_ref[8 * t + 3 * k : 8 * t + 3 * k + 3, :] = y
    for t, y in enumerate(split3(m)):
        m_ref[8 * t + 6 : 8 * t + 7, :] = y
    mt_ref[...] = m_ref[...].astype(BF16)

    def body(i, _):
        o = pl.multiple_of(i * LANES, LANES)
        x = b_ref[:, pl.ds(o, LANES)].astype(BF16)
        ys_ref[pl.ds(o, LANES), :] = jnp.concatenate([x, x, x, x], axis=0).T
        return 0

    lax.fori_loop(0, n // LANES, body, 0, unroll=4)


def fill_weights(p, v, wq_ref, wr_ref):
    n = p.shape[1]
    (pp, vv), (cc, dn, ce, gn) = basis(p, v)
    wq_ref[...] = jnp.zeros(wq_ref.shape, F32)
    wr_ref[...] = jnp.zeros(wr_ref.shape, F32)
    cc, dn, ce, gn = split3(cc), split3(dn + SOFTEN), split3(ce), split3(gn)
    for w in range(3):
        o = 32 * w
        for k in range(3):
            wq_ref[o + 3 * k : o + 3 * k + 3, :] = -2.0 * pp[w]
            wr_ref[o + 3 * k : o + 3 * k + 3, :] = -vv[w]
            wr_ref[o + 9 + 3 * k : o + 12 + 3 * k, :] = -pp[w]
        wq_ref[o + 18 : o + 19, :] = cc[w]
        wq_ref[o + 19 : o + 20, :] = dn[w]
        wr_ref[o + 18 : o + 19, :] = ce[w]
        wr_ref[o + 19 : o + 20, :] = gn[w]
    wq_ref[20:26, :] = jnp.ones((6, n), F32)
    wr_ref[26:32, :] = jnp.ones((6, n), F32)


def sweep_kernel(recv_ref, ys_ref, mt_ref, out_ref, act_ref, res_ref, wq_ref, wr_ref, wa_ref, wb_ref):
    lists = recv_ref.shape[0]
    stars = ys_ref.shape[0]
    lane = lax.broadcasted_iota(jnp.int32, (8, LANES), 1)
    act_ref[...] = jnp.zeros(act_ref.shape, F32)
    offsets = []
    total = jnp.int32(0)
    for k in range(lists):
        x = recv_ref[k]
        offsets.append(total)
        shift = total & (LANES - 1)
        o = pl.multiple_of((total >> 7) * LANES, LANES)
        x = pltpu.roll(x, shift, 1)
        act_ref[:, pl.ds(o, LANES)] += jnp.where(lane >= shift, x, 0.0)
        act_ref[:, pl.ds(o + LANES, LANES)] += jnp.where(lane < shift, x, 0.0)
        total = total + jnp.max(recv_ref[k, 6:7, :].astype(jnp.int32))
    size = wq_ref.shape[1]
    fill_weights(act_ref[0:3, 0:size], act_ref[3:6, 0:size], wq_ref, wr_ref)
    for w in (wa_ref, wb_ref):
        w[0] = wq_ref[...].astype(BF16)
        w[1] = wr_ref[...].astype(BF16)

    def dot(a, b):
        return jnp.dot(a, b, preferred_element_type=F32)

    def strengths(qr):
        q, rw = qr[:, :LANES], qr[:, LANES:]
        inv = lax.rsqrt(q)
        inv2 = inv * inv
        s = inv * inv2
        st = jnp.concatenate([s, s * inv2 * rw], axis=1)
        hi = st.astype(BF16)
        return hi, (st - hi.astype(F32)).astype(BF16)

    def store(cols, s, t):
        p, v = act_ref[0:3, cols], act_ref[3:6, cols]
        res_ref[0:3, cols] = s[0:3] - p * s[6:7]
        res_ref[3:6, cols] = s[3:6] - v * s[6:7] - 3.0 * (t[0:3] - p * t[6:7])

    def tile(t, _):
        cols = pl.ds(pl.multiple_of(t * LANES, LANES), LANES)
        half = stars // 2
        high, low = jnp.zeros((32, 2 * LANES), F32), jnp.zeros((16, 2 * LANES), F32)
        for h, w in enumerate((wa_ref, wb_ref)):
            rows = slice(h * half, (h + 1) * half)
            hi, lo = strengths(dot(ys_ref[rows, :], jnp.concatenate([w[0, :, cols], w[1, :, cols]], axis=1)))
            high = high + dot(mt_ref[:, rows], hi)
            low = low + dot(mt_ref[0:16, rows], lo)
        x = (high[16:24] + low[8:16]) + (high[8:16] + low[0:8]) + high[0:8]
        store(cols, x[:, :LANES], x[:, LANES:])
        return 0

    def narrow_tile(t, _):
        cols = pl.ds(pl.multiple_of(t * LANES, LANES), LANES)
        half = stars // 2
        first = lax.broadcasted_iota(jnp.int32, (LANES, LANES), 1) < LANES // 2
        weights = []
        for ref in (wq_ref, wr_ref):
            w = jnp.where(first, ref[:, cols], 0.0)
            weights.append(jnp.concatenate([w, pltpu.roll(w, LANES // 2, 1)], axis=0))
        w = jnp.concatenate(weights, axis=1).astype(BF16)
        high, low = jnp.zeros((64, 2 * LANES), F32), jnp.zeros((32, 2 * LANES), F32)
        for h in range(2):
            a = slice(h * half // 2, (h + 1) * half // 2)
            b = slice(half + h * half // 2, half + (h + 1) * half // 2)
            hi, lo = strengths(dot(jnp.concatenate([ys_ref[a, :], ys_ref[b, :]], axis=1), w))
            high = high + dot(jnp.concatenate([mt_ref[:, a], mt_ref[:, b]], axis=0), hi)
            low = low + dot(jnp.concatenate([mt_ref[0:16, a], mt_ref[0:16, b]], axis=0), lo)
        x = (high[16:24] + low[8:16]) + (high[8:16] + low[0:8]) + high[0:8]
        y = (high[48:56] + low[24:32]) + (high[40:48] + low[16:24]) + high[32:40]
        s = x[:, :LANES] + pltpu.roll(y[:, :LANES], LANES // 2, 1)
        t = x[:, LANES:] + pltpu.roll(y[:, LANES:], LANES // 2, 1)
        store(cols, s, t)
        return 0

    rest = total & (LANES - 1)
    whole = (total >> 7) + jnp.where(rest > LANES // 2, 1, 0)
    lax.fori_loop(0, whole, tile, 0)
    lax.fori_loop(whole, (total + (LANES - 1)) >> 7, narrow_tile, 0)
    for k in range(lists):
        shift = offsets[k] & (LANES - 1)
        o = pl.multiple_of((offsets[k] >> 7) * LANES, LANES)
        back = (LANES - shift) & (LANES - 1)
        a = pltpu.roll(res_ref[:, pl.ds(o, LANES)], back, 1)
        b = pltpu.roll(res_ref[:, pl.ds(o + LANES, LANES)], back, 1)
        out_ref[k] = jnp.where(lane < LANES - shift, a, b)


def finish_kernel(recv_ref, own_ref, out_ref):
    x = recv_ref[0]
    for k in range(1, recv_ref.shape[0]):
        x = x + recv_ref[k]
    new_acc, new_jerk = x[0:3, :CAP], x[3:6, :CAP]
    own = own_ref[:, :CAP]
    p, v, acc, jerk, e = own[0:3], own[3:6], own[6:9], own[9:12], own[12:13]
    change = acc - new_acc
    e2 = e * e
    e3 = e2 * e
    e4 = e2 * e2
    snap = (-6.0 * change - e * (4.0 * jerk + 2.0 * new_jerk)) / e2
    crackle = (12.0 * change + 6.0 * e * (jerk + new_jerk)) / e3
    pos = p + e4 / 24.0 * snap + e4 * e / 120.0 * crackle
    vel = v + e3 / 6.0 * snap + e4 / 24.0 * crackle
    live = lax.broadcasted_iota(jnp.int32, (3, CAP), 1).astype(F32) < own[13:14]
    for k, y in enumerate((pos, vel, new_acc, new_jerk)):
        y = jnp.where(live, y, 0.0)
        for c in range(3):
            out_ref[3 * k + c, 0] = y[c : c + 1]


def spec(space):
    return pl.BlockSpec(memory_space=space)


def params(limit=VMEM):
    return pltpu.CompilerParams(vmem_limit_bytes=limit)


def on_device(groups, field_pos, field_vel, field_acc, field_jerk, field_mass, levels, active_index, active_count):
    n = field_pos.shape[1]
    lists = len(groups[0])
    vmem = spec(pltpu.VMEM)
    send, own, pv = pl.pallas_call(
        select_kernel,
        out_shape=(
            jax.ShapeDtypeStruct((lists, 8, LANES), F32),
            jax.ShapeDtypeStruct((16, LANES), F32),
            jax.ShapeDtypeStruct((8, n), F32),
        ),
        in_specs=[spec(pltpu.HBM)] * 8,
        scratch_shapes=[pltpu.SMEM((1, 1, CAP), jnp.int32), pltpu.SMEM((1, 1), jnp.int32)]
        + [pltpu.VMEM((3, n), F32)] * 4
        + [pltpu.VMEM((1, n), F32), pltpu.VMEM((1, n), jnp.int32), pltpu.VMEM((16, n), F32)]
        + [pltpu.SemaphoreType.DMA((8,))],
        compiler_params=params(),
        cost_estimate=pl.CostEstimate(flops=1 << 20, bytes_accessed=1 << 20, transcendentals=0),
        name="select",
    )(active_count, *[
        pltpu.with_memory_space_constraint(x, pltpu.HBM)
        for x in (
            active_index, field_pos, field_vel, field_acc, field_jerk,
            field_mass.reshape(1, n), levels.reshape(1, n),
        )
    ])
    axes = ("blk", "act")
    recv = lax.all_to_all(send, axes, 0, 0, axis_index_groups=groups, tiled=True)
    ys, mt = pl.pallas_call(
        prepare_kernel,
        out_shape=(jax.ShapeDtypeStruct((n, LANES), BF16), jax.ShapeDtypeStruct((32, n), BF16)),
        in_specs=[vmem],
        scratch_shapes=[pltpu.VMEM((32, n), F32)] * 2,
        compiler_params=params(),
        cost_estimate=pl.CostEstimate(flops=1 << 22, bytes_accessed=4 << 20, transcendentals=0),
        name="prepare",
    )(pv)
    size = lists * CAP
    part = pl.pallas_call(
        sweep_kernel,
        out_shape=jax.ShapeDtypeStruct((lists, 8, LANES), F32),
        in_specs=[vmem] * 3,
        scratch_shapes=[pltpu.VMEM((8, size + LANES), F32)] * 2
        + [pltpu.VMEM((LANES, size), F32)] * 2
        + [pltpu.VMEM((2, LANES, size), BF16)] * 2,
        compiler_params=params(),
        cost_estimate=pl.CostEstimate(flops=10 << 30, bytes_accessed=4 << 20, transcendentals=0),
        name="sweep",
    )(recv, ys, mt)
    back = lax.all_to_all(part, axes, 0, 0, axis_index_groups=groups, tiled=True)
    out = pl.pallas_call(
        finish_kernel,
        out_shape=jax.ShapeDtypeStruct((12, 1, 1, CAP), F32),
        in_specs=[vmem, vmem],
        compiler_params=params(),
        name="finish",
    )(back, own)
    return out


def list_groups():
    groups = []
    for y in range(4):
        for flip in range(2):
            group = []
            for b in range(16):
                z_hi = (b >> 1) & 1
                z_lo = z_hi ^ flip
                group.append(b * 8 + z_lo * 4 + y)
            groups.append(group)
    return groups


def solution(mesh):
    return jax.shard_map(
        functools.partial(on_device, list_groups()),
        mesh=mesh,
        in_specs=(
            P(None, "blk"),
            P(None, "blk"),
            P(None, "blk"),
            P(None, "blk"),
            P("blk"),
            P("blk"),
            P("blk", "act", None),
            P("blk", "act"),
        ),
        out_specs=P(None, "blk", "act", None),
        check_vma=False,
    )
```

```python
import functools

import jax
import jax.numpy as jnp
from jax import lax
from jax.experimental import pallas as pl
from jax.experimental.pallas import tpu as pltpu
from jax.sharding import PartitionSpec as P

F32 = jnp.float32
BF16 = jnp.bfloat16
SOFTEN = 0.01
NOW = 11
TICK = 0.0625
GRID = 16.0
LANES = 128
CAP = 64
VMEM = 44 << 20


def round_bf16(x):
    return x.astype(BF16).astype(F32)


def split2(x):
    a = round_bf16(x)
    return a, round_bf16(x - a)


def split3(x):
    a = round_bf16(x)
    b = round_bf16(x - a)
    return a, b, x - a - b


def coarse(x):
    c = round_bf16(jnp.round(x * GRID) * (1.0 / GRID))
    return c, x - c


def rows_sum(x):
    return jnp.sum(x, axis=0, keepdims=True)


def basis(p, v):
    c, d = coarse(p)
    e, f = coarse(v)
    parts = (c, *split2(d)), (e, *split2(f))
    norms = (
        rows_sum(c * c),
        rows_sum(2.0 * c * d + d * d),
        rows_sum(c * e),
        rows_sum(c * f + d * e + d * f),
    )
    return parts, norms


def select_kernel(
    cnt_hbm, idx_hbm, pos_hbm, vel_hbm, acc_hbm, jerk_hbm, mass_hbm, lev_hbm,
    send_ref, own_ref, pv_ref, idx, cnt, pos, vel, acc, jerk, mass, lev, table, sem,
):
    pairs = (
        (lev_hbm, lev), (pos_hbm, pos), (vel_hbm, vel), (acc_hbm, acc), (jerk_hbm, jerk), (mass_hbm, mass),
        (idx_hbm, idx), (cnt_hbm, cnt),
    )
    copies = [pltpu.make_async_copy(a, b, sem.at[k]) for k, (a, b) in enumerate(pairs)]
    for copy in copies:
        copy.start()
    for copy in copies:
        copy.wait()
    level = lev[...]
    e = (NOW & (jnp.left_shift(jnp.ones_like(level), 4 - level) - 1)).astype(F32) * TICK
    x, u, a, j = pos[...], vel[...], acc[...], jerk[...]
    p = x + e * (u + e * (a * 0.5 + e * j / 6.0))
    v = u + e * (a + e * j * 0.5)
    pv_ref[0:3, :] = p
    pv_ref[3:6, :] = v
    pv_ref[6:7, :] = mass[...]
    table[0:3, :] = p
    table[3:6, :] = v
    table[6:9, :] = a
    table[9:12, :] = j
    table[12:13, :] = e
    lane = lax.broadcasted_iota(jnp.int32, (16, LANES), 1)
    got = jnp.zeros((16, LANES), F32)
    for s in range(CAP):
        i = idx[0, 0, s]
        block = table[:, pl.ds(pl.multiple_of((i >> 7) * LANES, LANES), LANES)]
        got = jnp.where(lane == s, pltpu.roll(block, (s - i) & (LANES - 1), 1), got)
    count = cnt[0, 0]
    own_ref[0:13, :] = got[0:13]
    own_ref[13:16, :] = jnp.full((3, LANES), count.astype(F32))
    row = lax.broadcasted_iota(jnp.int32, (8, LANES), 0)
    live = lax.broadcasted_iota(jnp.int32, (8, LANES), 1) < count
    out = jnp.where(row < 6, jnp.where(live, got[0:8], 0.0), jnp.where(row == 6, count.astype(F32), 0.0))
    for k in range(send_ref.shape[0]):
        send_ref[k] = out


def prepare_kernel(pv_ref, ys_ref, mt_ref, b_ref, m_ref):
    n = pv_ref.shape[1]
    p, v, m = pv_ref[0:3, :], pv_ref[3:6, :], pv_ref[6:7, :]
    (pp, vv), norms = basis(p, v)
    for k, x in enumerate((*pp, *vv)):
        b_ref[3 * k : 3 * k + 3, :] = x
    b_ref[18:20, :] = jnp.ones((2, n), F32)
    for k, x in enumerate(norms):
        for t, y in enumerate(split3(x)):
            b_ref[20 + 3 * k + t : 21 + 3 * k + t, :] = y
    m_ref[...] = jnp.zeros(m_ref.shape, F32)
    for k, x in enumerate((m * p, m * v)):
        for t, y in enumerate(split3(x)):
            m_ref[8 * t + 3 * k : 8 * t + 3 * k + 3, :] = y
    for t, y in enumerate(split3(m)):
        m_ref[8 * t + 6 : 8 * t + 7, :] = y
    mt_ref[...] = m_ref[...].astype(BF16)

    def body(i, _):
        o = pl.multiple_of(i * LANES, LANES)
        x = b_ref[:, pl.ds(o, LANES)].astype(BF16)
        ys_ref[pl.ds(o, LANES), :] = jnp.concatenate([x, x, x, x], axis=0).T
        return 0

    lax.fori_loop(0, n // LANES, body, 0, unroll=4)


def fill_weights(p, v, wq_ref, wr_ref):
    n = p.shape[1]
    (pp, vv), (cc, dn, ce, gn) = basis(p, v)
    wq_ref[...] = jnp.zeros(wq_ref.shape, F32)
    wr_ref[...] = jnp.zeros(wr_ref.shape, F32)
    cc, dn, ce, gn = split3(cc), split3(dn + SOFTEN), split3(ce), split3(gn)
    for w in range(3):
        o = 32 * w
        for k in range(3):
            wq_ref[o + 3 * k : o + 3 * k + 3, :] = -2.0 * pp[w]
            wr_ref[o + 3 * k : o + 3 * k + 3, :] = -vv[w]
            wr_ref[o + 9 + 3 * k : o + 12 + 3 * k, :] = -pp[w]
        wq_ref[o + 18 : o + 19, :] = cc[w]
        wq_ref[o + 19 : o + 20, :] = dn[w]
        wr_ref[o + 18 : o + 19, :] = ce[w]
        wr_ref[o + 19 : o + 20, :] = gn[w]
    wq_ref[20:26, :] = jnp.ones((6, n), F32)
    wr_ref[26:32, :] = jnp.ones((6, n), F32)


def sweep_kernel(recv_ref, ys_ref, mt_ref, out_ref, act_ref, res_ref, wq_ref, wr_ref, w_ref):
    lists = recv_ref.shape[0]
    stars = ys_ref.shape[0]
    lane = lax.broadcasted_iota(jnp.int32, (8, LANES), 1)
    act_ref[...] = jnp.zeros(act_ref.shape, F32)
    offsets = []
    total = jnp.int32(0)
    chunk = jnp.zeros((8, LANES), F32)
    for k in range(lists):
        offsets.append(total)
        shift = total & (LANES - 1)
        o = pl.multiple_of((total >> 7) * LANES, LANES)
        x = pltpu.roll(recv_ref[k], shift, 1)
        chunk = chunk + jnp.where(lane >= shift, x, 0.0)
        act_ref[:, pl.ds(o, LANES)] = chunk
        total = total + jnp.max(recv_ref[k, 6:7, :].astype(jnp.int32))
        full = (total >> 7) * LANES > o
        chunk = jnp.where(full, jnp.where(lane < shift, x, 0.0), chunk)
    act_ref[:, pl.ds(pl.multiple_of((total >> 7) * LANES, LANES), LANES)] = chunk
    size = wq_ref.shape[1]
    common = size * 5 // 8

    def ready(lo, hi):
        cols = slice(lo, hi)
        fill_weights(act_ref[0:3, cols], act_ref[3:6, cols], wq_ref.at[:, cols], wr_ref.at[:, cols])
        w_ref[0, :, cols] = wq_ref[:, cols].astype(BF16)
        w_ref[1, :, cols] = wr_ref[:, cols].astype(BF16)

    ready(0, common)
    pl.when(total > common)(lambda: ready(common, size))

    def dot(a, b):
        return jnp.dot(a, b, preferred_element_type=F32)

    def strengths(qr):
        q, rw = qr[:, :LANES], qr[:, LANES:]
        inv = lax.rsqrt(q)
        inv2 = inv * inv
        s = inv * inv2
        st = jnp.concatenate([s, s * inv2 * rw], axis=1)
        hi = st.astype(BF16)
        return hi, (st - hi.astype(F32)).astype(BF16)

    def store(cols, s, t):
        p, v = act_ref[0:3, cols], act_ref[3:6, cols]
        res_ref[0:3, cols] = s[0:3] - p * s[6:7]
        res_ref[3:6, cols] = s[3:6] - v * s[6:7] - 3.0 * (t[0:3] - p * t[6:7])

    def tile(t, _):
        cols = pl.ds(pl.multiple_of(t * LANES, LANES), LANES)
        half = stars // 2
        high, low = jnp.zeros((32, 2 * LANES), F32), jnp.zeros((16, 2 * LANES), F32)
        w = jnp.concatenate([w_ref[0, :, cols], w_ref[1, :, cols]], axis=1)
        for h in range(2):
            rows = slice(h * half, (h + 1) * half)
            hi, lo = strengths(dot(ys_ref[rows, :], w))
            high = high + dot(mt_ref[:, rows], hi)
            low = low + dot(mt_ref[0:16, rows], lo)
        x = (high[16:24] + low[8:16]) + (high[8:16] + low[0:8]) + high[0:8]
        store(cols, x[:, :LANES], x[:, LANES:])
        return 0

    def narrow_tile(t, _):
        cols = pl.ds(pl.multiple_of(t * LANES, LANES), LANES)
        half = stars // 2
        first = lax.broadcasted_iota(jnp.int32, (LANES, LANES), 1) < LANES // 2
        weights = []
        for ref in (wq_ref, wr_ref):
            w = jnp.where(first, ref[:, cols], 0.0)
            weights.append(jnp.concatenate([w, pltpu.roll(w, LANES // 2, 1)], axis=0))
        w = jnp.concatenate(weights, axis=1).astype(BF16)
        high, low = jnp.zeros((64, 2 * LANES), F32), jnp.zeros((32, 2 * LANES), F32)
        for h in range(2):
            a = slice(h * half // 2, (h + 1) * half // 2)
            b = slice(half + h * half // 2, half + (h + 1) * half // 2)
            hi, lo = strengths(dot(jnp.concatenate([ys_ref[a, :], ys_ref[b, :]], axis=1), w))
            high = high + dot(jnp.concatenate([mt_ref[:, a], mt_ref[:, b]], axis=0), hi)
            low = low + dot(jnp.concatenate([mt_ref[0:16, a], mt_ref[0:16, b]], axis=0), lo)
        x = (high[16:24] + low[8:16]) + (high[8:16] + low[0:8]) + high[0:8]
        y = (high[48:56] + low[24:32]) + (high[40:48] + low[16:24]) + high[32:40]
        s = x[:, :LANES] + pltpu.roll(y[:, :LANES], LANES // 2, 1)
        t = x[:, LANES:] + pltpu.roll(y[:, LANES:], LANES // 2, 1)
        store(cols, s, t)
        return 0

    rest = total & (LANES - 1)
    whole = (total >> 7) + jnp.where(rest > LANES // 2, 1, 0)
    lax.fori_loop(0, whole, tile, 0)
    lax.fori_loop(whole, (total + (LANES - 1)) >> 7, narrow_tile, 0)
    for k in range(lists):
        shift = offsets[k] & (LANES - 1)
        o = pl.multiple_of((offsets[k] >> 7) * LANES, LANES)
        back = (LANES - shift) & (LANES - 1)
        a = pltpu.roll(res_ref[:, pl.ds(o, LANES)], back, 1)
        b = pltpu.roll(res_ref[:, pl.ds(o + LANES, LANES)], back, 1)
        out_ref[k] = jnp.where(lane < LANES - shift, a, b)


def finish_kernel(recv_ref, own_ref, out_ref):
    x = recv_ref[0]
    for k in range(1, recv_ref.shape[0]):
        x = x + recv_ref[k]
    new_acc, new_jerk = x[0:3, :CAP], x[3:6, :CAP]
    own = own_ref[:, :CAP]
    p, v, acc, jerk, e = own[0:3], own[3:6], own[6:9], own[9:12], own[12:13]
    change = acc - new_acc
    e2 = e * e
    e3 = e2 * e
    e4 = e2 * e2
    snap = (-6.0 * change - e * (4.0 * jerk + 2.0 * new_jerk)) / e2
    crackle = (12.0 * change + 6.0 * e * (jerk + new_jerk)) / e3
    pos = p + e4 / 24.0 * snap + e4 * e / 120.0 * crackle
    vel = v + e3 / 6.0 * snap + e4 / 24.0 * crackle
    live = lax.broadcasted_iota(jnp.int32, (3, CAP), 1).astype(F32) < own[13:14]
    for k, y in enumerate((pos, vel, new_acc, new_jerk)):
        y = jnp.where(live, y, 0.0)
        for c in range(3):
            out_ref[3 * k + c, 0] = y[c : c + 1]


def spec(space):
    return pl.BlockSpec(memory_space=space)


def params(limit=VMEM):
    return pltpu.CompilerParams(vmem_limit_bytes=limit)


def on_device(groups, field_pos, field_vel, field_acc, field_jerk, field_mass, levels, active_index, active_count):
    n = field_pos.shape[1]
    lists = len(groups[0])
    vmem = spec(pltpu.VMEM)
    send, own, pv = pl.pallas_call(
        select_kernel,
        out_shape=(
            jax.ShapeDtypeStruct((lists, 8, LANES), F32),
            jax.ShapeDtypeStruct((16, LANES), F32),
            jax.ShapeDtypeStruct((8, n), F32),
        ),
        in_specs=[spec(pltpu.HBM)] * 8,
        scratch_shapes=[pltpu.SMEM((1, 1, CAP), jnp.int32), pltpu.SMEM((1, 1), jnp.int32)]
        + [pltpu.VMEM((3, n), F32)] * 4
        + [pltpu.VMEM((1, n), F32), pltpu.VMEM((1, n), jnp.int32), pltpu.VMEM((16, n), F32)]
        + [pltpu.SemaphoreType.DMA((8,))],
        compiler_params=params(),
        cost_estimate=pl.CostEstimate(flops=1 << 20, bytes_accessed=1 << 20, transcendentals=0),
        name="select",
    )(active_count, *[
        pltpu.with_memory_space_constraint(x, pltpu.HBM)
        for x in (
            active_index, field_pos, field_vel, field_acc, field_jerk,
            field_mass.reshape(1, n), levels.reshape(1, n),
        )
    ])
    axes = ("blk", "act")
    recv = lax.all_to_all(send, axes, 0, 0, axis_index_groups=groups, tiled=True)
    ys, mt = pl.pallas_call(
        prepare_kernel,
        out_shape=(jax.ShapeDtypeStruct((n, LANES), BF16), jax.ShapeDtypeStruct((32, n), BF16)),
        in_specs=[vmem],
        scratch_shapes=[pltpu.VMEM((32, n), F32)] * 2,
        compiler_params=params(),
        cost_estimate=pl.CostEstimate(flops=1 << 22, bytes_accessed=4 << 20, transcendentals=0),
        name="prepare",
    )(pv)
    size = lists * CAP
    part = pl.pallas_call(
        sweep_kernel,
        out_shape=jax.ShapeDtypeStruct((lists, 8, LANES), F32),
        in_specs=[vmem] * 3,
        scratch_shapes=[pltpu.VMEM((8, size + LANES), F32)] * 2
        + [pltpu.VMEM((LANES, size), F32)] * 2
        + [pltpu.VMEM((2, LANES, size), BF16)],
        compiler_params=params(),
        cost_estimate=pl.CostEstimate(flops=10 << 30, bytes_accessed=4 << 20, transcendentals=0),
        name="sweep",
    )(recv, ys, mt)
    back = lax.all_to_all(part, axes, 0, 0, axis_index_groups=groups, tiled=True)
    out = pl.pallas_call(
        finish_kernel,
        out_shape=jax.ShapeDtypeStruct((12, 1, 1, CAP), F32),
        in_specs=[vmem, vmem],
        compiler_params=params(),
        name="finish",
    )(back, own)
    return out


def list_groups():
    groups = []
    for y in range(4):
        for flip in range(2):
            group = []
            for b in range(16):
                z_hi = (b >> 1) & 1
                z_lo = z_hi ^ flip
                group.append(b * 8 + z_lo * 4 + y)
            groups.append(group)
    return groups


def solution(mesh):
    return jax.shard_map(
        functools.partial(on_device, list_groups()),
        mesh=mesh,
        in_specs=(
            P(None, "blk"),
            P(None, "blk"),
            P(None, "blk"),
            P(None, "blk"),
            P("blk"),
            P("blk"),
            P("blk", "act", None),
            P("blk", "act"),
        ),
        out_specs=P(None, "blk", "act", None),
        check_vma=False,
    )
```

```python
import functools

import jax
import jax.numpy as jnp
from jax import lax
from jax.experimental import pallas as pl
from jax.experimental.pallas import tpu as pltpu
from jax.sharding import PartitionSpec as P

F32 = jnp.float32
BF16 = jnp.bfloat16
SOFTEN = 0.01
NOW = 11
TICK = 0.0625
GRID = 16.0
LANES = 128
CAP = 64
FINE = 16
VMEM = 44 << 20


def round_bf16(x):
    return x.astype(BF16).astype(F32)


def split2(x):
    a = round_bf16(x)
    return a, round_bf16(x - a)


def split3(x):
    a = round_bf16(x)
    b = round_bf16(x - a)
    return a, b, x - a - b


def coarse(x):
    c = round_bf16(jnp.round(x * GRID) * (1.0 / GRID))
    return c, x - c


def rows_sum(x):
    return jnp.sum(x, axis=0, keepdims=True)


def basis(p, v):
    c, d = coarse(p)
    e, f = coarse(v)
    parts = (c, *split2(d)), (e, *split2(f))
    norms = (
        rows_sum(c * c),
        rows_sum(2.0 * c * d + d * d),
        rows_sum(c * e),
        rows_sum(c * f + d * e + d * f),
    )
    return parts, norms


def select_kernel(
    cnt_hbm, idx_hbm, pos_hbm, vel_hbm, acc_hbm, jerk_hbm, mass_hbm, lev_hbm,
    send_ref, own_ref, pv_ref, idx, cnt, pos, vel, acc, jerk, mass, lev, table, sem,
):
    pairs = (
        (lev_hbm, lev), (pos_hbm, pos), (vel_hbm, vel), (acc_hbm, acc), (jerk_hbm, jerk), (mass_hbm, mass),
        (idx_hbm, idx), (cnt_hbm, cnt),
    )
    copies = [pltpu.make_async_copy(a, b, sem.at[k]) for k, (a, b) in enumerate(pairs)]
    for copy in copies:
        copy.start()
    for copy in copies:
        copy.wait()
    level = lev[...]
    e = (NOW & (jnp.left_shift(jnp.ones_like(level), 4 - level) - 1)).astype(F32) * TICK
    x, u, a, j = pos[...], vel[...], acc[...], jerk[...]
    p = x + e * (u + e * (a * 0.5 + e * j / 6.0))
    v = u + e * (a + e * j * 0.5)
    pv_ref[0:3, :] = p
    pv_ref[3:6, :] = v
    pv_ref[6:7, :] = mass[...]
    table[0:3, :] = p
    table[3:6, :] = v
    table[6:9, :] = a
    table[9:12, :] = j
    table[12:13, :] = e
    lane = lax.broadcasted_iota(jnp.int32, (16, LANES), 1)
    got = jnp.zeros((16, LANES), F32)
    for s in range(CAP):
        i = idx[0, 0, s]
        block = table[:, pl.ds(pl.multiple_of((i >> 7) * LANES, LANES), LANES)]
        got = jnp.where(lane == s, pltpu.roll(block, (s - i) & (LANES - 1), 1), got)
    count = cnt[0, 0]
    own_ref[0:13, :] = got[0:13]
    own_ref[13:16, :] = jnp.full((3, LANES), count.astype(F32))
    row = lax.broadcasted_iota(jnp.int32, (8, LANES), 0)
    live = lax.broadcasted_iota(jnp.int32, (8, LANES), 1) < count
    out = jnp.where(row < 6, jnp.where(live, got[0:8], 0.0), jnp.where(row == 6, count.astype(F32), 0.0))
    for k in range(send_ref.shape[0]):
        send_ref[k] = out


def prepare_kernel(pv_ref, ys_ref, mt_ref, b_ref, m_ref):
    n = pv_ref.shape[1]
    p, v, m = pv_ref[0:3, :], pv_ref[3:6, :], pv_ref[6:7, :]
    (pp, vv), norms = basis(p, v)
    cc, dn, ce, gn = (split3(x) for x in norms)
    ones = jnp.ones((4, n), F32)
    b_ref[0:3, :] = pp[0]
    b_ref[3:6, :] = vv[0]
    for t in range(3):
        b_ref[6 + t : 7 + t, :] = cc[t]
        b_ref[9 + t : 10 + t, :] = ce[t]
    b_ref[12:16, :] = ones
    for k, x in enumerate((*pp, *vv)):
        b_ref[FINE + 3 * k : FINE + 3 * k + 3, :] = x
    b_ref[FINE + 18 : FINE + 20, :] = ones[0:2]
    for t in range(3):
        b_ref[FINE + 20 + t : FINE + 21 + t, :] = dn[t]
        b_ref[FINE + 23 + t : FINE + 24 + t, :] = gn[t]
    b_ref[FINE + 26 : FINE + 32, :] = jnp.zeros((6, n), F32)
    m_ref[...] = jnp.zeros(m_ref.shape, F32)
    for k, x in enumerate((m * p, m * v)):
        for t, y in enumerate(split3(x)):
            m_ref[8 * t + 3 * k : 8 * t + 3 * k + 3, :] = y
    for t, y in enumerate(split3(m)):
        m_ref[8 * t + 6 : 8 * t + 7, :] = y
    mt_ref[...] = m_ref[...].astype(BF16)

    def body(i, _):
        o = pl.multiple_of(i * LANES, LANES)
        x = b_ref[0:FINE, pl.ds(o, LANES)].astype(BF16)
        y = b_ref[FINE : FINE + 32, pl.ds(o, LANES)].astype(BF16)
        ys_ref[pl.ds(o, LANES), :] = jnp.concatenate([x, y, y, y, x], axis=0).T
        return 0

    lax.fori_loop(0, n // LANES, body, 0, unroll=4)


def fill_weights(p, v, wq_ref, wr_ref):
    n = p.shape[1]
    (pp, vv), norms = basis(p, v)
    cc, dn, ce, gn = norms
    cc, dn, ce, gn = split3(cc), split3(dn + SOFTEN), split3(ce), split3(gn)
    wq_ref[...] = jnp.zeros(wq_ref.shape, F32)
    wr_ref[...] = jnp.zeros(wr_ref.shape, F32)
    ones = jnp.ones((3, n), F32)
    wq_ref[0:3, :] = -2.0 * pp[0]
    wr_ref[0:3, :] = -vv[0]
    wr_ref[3:6, :] = -pp[0]
    wq_ref[6:9, :] = ones
    wr_ref[9:12, :] = ones
    for w in range(3):
        wq_ref[12 + w : 13 + w, :] = cc[w]
        wr_ref[12 + w : 13 + w, :] = ce[w]
        o = FINE + 32 * w
        for k in range(3):
            if w or k:
                wq_ref[o + 3 * k : o + 3 * k + 3, :] = -2.0 * pp[w]
                wr_ref[o + 3 * k : o + 3 * k + 3, :] = -vv[w]
                wr_ref[o + 9 + 3 * k : o + 12 + 3 * k, :] = -pp[w]
        wq_ref[o + 18 : o + 19, :] = dn[w]
        wr_ref[o + 18 : o + 19, :] = gn[w]
    wq_ref[FINE + 20 : FINE + 23, :] = ones
    wr_ref[FINE + 23 : FINE + 26, :] = ones


def sweep_kernel(recv_ref, ys_ref, mt_ref, out_ref, act_ref, res_ref, wq_ref, wr_ref, w_ref):
    lists = recv_ref.shape[0]
    stars = ys_ref.shape[0]
    lane = lax.broadcasted_iota(jnp.int32, (8, LANES), 1)
    act_ref[...] = jnp.zeros(act_ref.shape, F32)
    offsets = []
    total = jnp.int32(0)
    chunk = jnp.zeros((8, LANES), F32)
    for k in range(lists):
        offsets.append(total)
        shift = total & (LANES - 1)
        o = pl.multiple_of((total >> 7) * LANES, LANES)
        x = pltpu.roll(recv_ref[k], shift, 1)
        chunk = chunk + jnp.where(lane >= shift, x, 0.0)
        act_ref[:, pl.ds(o, LANES)] = chunk
        total = total + jnp.max(recv_ref[k, 6:7, :].astype(jnp.int32))
        full = (total >> 7) * LANES > o
        chunk = jnp.where(full, jnp.where(lane < shift, x, 0.0), chunk)
    act_ref[:, pl.ds(pl.multiple_of((total >> 7) * LANES, LANES), LANES)] = chunk
    size = wq_ref.shape[1]
    common = size * 5 // 8

    def ready(lo, hi):
        cols = slice(lo, hi)
        fill_weights(act_ref[0:3, cols], act_ref[3:6, cols], wq_ref.at[:, cols], wr_ref.at[:, cols])
        w_ref[0, :, cols] = wq_ref[:, cols].astype(BF16)
        w_ref[1, :, cols] = wr_ref[:, cols].astype(BF16)

    ready(0, common)
    pl.when(total > common)(lambda: ready(common, size))

    def dot(a, b):
        return jnp.dot(a, b, preferred_element_type=F32)

    def strengths(qr):
        q, rw = qr[:, :LANES], qr[:, LANES:]
        inv = lax.rsqrt(q)
        inv2 = inv * inv
        s = inv * inv2
        st = jnp.concatenate([s, s * inv2 * rw], axis=1)
        hi = st.astype(BF16)
        return hi, (st - hi.astype(F32)).astype(BF16)

    def store(cols, s, t):
        p, v = act_ref[0:3, cols], act_ref[3:6, cols]
        res_ref[0:3, cols] = s[0:3] - p * s[6:7]
        res_ref[3:6, cols] = s[3:6] - v * s[6:7] - 3.0 * (t[0:3] - p * t[6:7])

    def tile(t, _):
        cols = pl.ds(pl.multiple_of(t * LANES, LANES), LANES)
        half = stars // 2
        high, low = jnp.zeros((32, 2 * LANES), F32), jnp.zeros((16, 2 * LANES), F32)
        w = jnp.concatenate([w_ref[0, :, cols], w_ref[1, :, cols]], axis=1)
        for h in range(2):
            rows = slice(h * half, (h + 1) * half)
            hi, lo = strengths(dot(ys_ref[rows, :], w))
            high = high + dot(mt_ref[:, rows], hi)
            low = low + dot(mt_ref[0:16, rows], lo)
        x = (high[16:24] + low[8:16]) + (high[8:16] + low[0:8]) + high[0:8]
        store(cols, x[:, :LANES], x[:, LANES:])
        return 0

    def narrow_tile(t, _):
        cols = pl.ds(pl.multiple_of(t * LANES, LANES), LANES)
        half = stars // 2
        first = lax.broadcasted_iota(jnp.int32, (LANES, LANES), 1) < LANES // 2
        weights = []
        for ref in (wq_ref, wr_ref):
            w = jnp.where(first, ref[:, cols], 0.0)
            weights.append(jnp.concatenate([w, pltpu.roll(w, LANES // 2, 1)], axis=0))
        w = jnp.concatenate(weights, axis=1).astype(BF16)
        high, low = jnp.zeros((64, 2 * LANES), F32), jnp.zeros((32, 2 * LANES), F32)
        for h in range(2):
            a = slice(h * half // 2, (h + 1) * half // 2)
            b = slice(half + h * half // 2, half + (h + 1) * half // 2)
            hi, lo = strengths(dot(jnp.concatenate([ys_ref[a, :], ys_ref[b, :]], axis=1), w))
            high = high + dot(jnp.concatenate([mt_ref[:, a], mt_ref[:, b]], axis=0), hi)
            low = low + dot(jnp.concatenate([mt_ref[0:16, a], mt_ref[0:16, b]], axis=0), lo)
        x = (high[16:24] + low[8:16]) + (high[8:16] + low[0:8]) + high[0:8]
        y = (high[48:56] + low[24:32]) + (high[40:48] + low[16:24]) + high[32:40]
        s = x[:, :LANES] + pltpu.roll(y[:, :LANES], LANES // 2, 1)
        t = x[:, LANES:] + pltpu.roll(y[:, LANES:], LANES // 2, 1)
        store(cols, s, t)
        return 0

    rest = total & (LANES - 1)
    whole = (total >> 7) + jnp.where(rest > LANES // 2, 1, 0)
    lax.fori_loop(0, whole, tile, 0)
    lax.fori_loop(whole, (total + (LANES - 1)) >> 7, narrow_tile, 0)
    for k in range(lists):
        shift = offsets[k] & (LANES - 1)
        o = pl.multiple_of((offsets[k] >> 7) * LANES, LANES)
        back = (LANES - shift) & (LANES - 1)
        a = pltpu.roll(res_ref[:, pl.ds(o, LANES)], back, 1)
        b = pltpu.roll(res_ref[:, pl.ds(o + LANES, LANES)], back, 1)
        out_ref[k] = jnp.where(lane < LANES - shift, a, b)


def finish_kernel(recv_ref, own_ref, out_ref):
    x = recv_ref[0]
    for k in range(1, recv_ref.shape[0]):
        x = x + recv_ref[k]
    new_acc, new_jerk = x[0:3, :CAP], x[3:6, :CAP]
    own = own_ref[:, :CAP]
    p, v, acc, jerk, e = own[0:3], own[3:6], own[6:9], own[9:12], own[12:13]
    change = acc - new_acc
    e2 = e * e
    e3 = e2 * e
    e4 = e2 * e2
    snap = (-6.0 * change - e * (4.0 * jerk + 2.0 * new_jerk)) / e2
    crackle = (12.0 * change + 6.0 * e * (jerk + new_jerk)) / e3
    pos = p + e4 / 24.0 * snap + e4 * e / 120.0 * crackle
    vel = v + e3 / 6.0 * snap + e4 / 24.0 * crackle
    live = lax.broadcasted_iota(jnp.int32, (3, CAP), 1).astype(F32) < own[13:14]
    for k, y in enumerate((pos, vel, new_acc, new_jerk)):
        y = jnp.where(live, y, 0.0)
        for c in range(3):
            out_ref[3 * k + c, 0] = y[c : c + 1]


def spec(space):
    return pl.BlockSpec(memory_space=space)


def params(limit=VMEM):
    return pltpu.CompilerParams(vmem_limit_bytes=limit)


def on_device(groups, field_pos, field_vel, field_acc, field_jerk, field_mass, levels, active_index, active_count):
    n = field_pos.shape[1]
    lists = len(groups[0])
    vmem = spec(pltpu.VMEM)
    send, own, pv = pl.pallas_call(
        select_kernel,
        out_shape=(
            jax.ShapeDtypeStruct((lists, 8, LANES), F32),
            jax.ShapeDtypeStruct((16, LANES), F32),
            jax.ShapeDtypeStruct((8, n), F32),
        ),
        in_specs=[spec(pltpu.HBM)] * 8,
        scratch_shapes=[pltpu.SMEM((1, 1, CAP), jnp.int32), pltpu.SMEM((1, 1), jnp.int32)]
        + [pltpu.VMEM((3, n), F32)] * 4
        + [pltpu.VMEM((1, n), F32), pltpu.VMEM((1, n), jnp.int32), pltpu.VMEM((16, n), F32)]
        + [pltpu.SemaphoreType.DMA((8,))],
        compiler_params=params(),
        cost_estimate=pl.CostEstimate(flops=1 << 20, bytes_accessed=1 << 20, transcendentals=0),
        name="select",
    )(active_count, *[
        pltpu.with_memory_space_constraint(x, pltpu.HBM)
        for x in (
            active_index, field_pos, field_vel, field_acc, field_jerk,
            field_mass.reshape(1, n), levels.reshape(1, n),
        )
    ])
    axes = ("blk", "act")
    recv = lax.all_to_all(send, axes, 0, 0, axis_index_groups=groups, tiled=True)
    ys, mt = pl.pallas_call(
        prepare_kernel,
        out_shape=(jax.ShapeDtypeStruct((n, LANES), BF16), jax.ShapeDtypeStruct((32, n), BF16)),
        in_specs=[vmem],
        scratch_shapes=[pltpu.VMEM((FINE + 32, n), F32), pltpu.VMEM((32, n), F32)],
        compiler_params=params(),
        cost_estimate=pl.CostEstimate(flops=1 << 22, bytes_accessed=4 << 20, transcendentals=0),
        name="prepare",
    )(pv)
    size = lists * CAP
    part = pl.pallas_call(
        sweep_kernel,
        out_shape=jax.ShapeDtypeStruct((lists, 8, LANES), F32),
        in_specs=[vmem] * 3,
        scratch_shapes=[pltpu.VMEM((8, size + LANES), F32)] * 2
        + [pltpu.VMEM((LANES, size), F32)] * 2
        + [pltpu.VMEM((2, LANES, size), BF16)],
        compiler_params=params(),
        cost_estimate=pl.CostEstimate(flops=10 << 30, bytes_accessed=4 << 20, transcendentals=0),
        name="sweep",
    )(recv, ys, mt)
    back = lax.all_to_all(part, axes, 0, 0, axis_index_groups=groups, tiled=True)
    out = pl.pallas_call(
        finish_kernel,
        out_shape=jax.ShapeDtypeStruct((12, 1, 1, CAP), F32),
        in_specs=[vmem, vmem],
        compiler_params=params(),
        name="finish",
    )(back, own)
    return out


def list_groups():
    groups = []
    for y in range(4):
        for flip in range(2):
            group = []
            for b in range(16):
                z_hi = (b >> 1) & 1
                z_lo = z_hi ^ flip
                group.append(b * 8 + z_lo * 4 + y)
            groups.append(group)
    return groups


def solution(mesh):
    return jax.shard_map(
        functools.partial(on_device, list_groups()),
        mesh=mesh,
        in_specs=(
            P(None, "blk"),
            P(None, "blk"),
            P(None, "blk"),
            P(None, "blk"),
            P("blk"),
            P("blk"),
            P("blk", "act", None),
            P("blk", "act"),
        ),
        out_specs=P(None, "blk", "act", None),
        check_vma=False,
    )
```

```python
import functools

import jax
import jax.numpy as jnp
from jax import lax
from jax.experimental import pallas as pl
from jax.experimental.pallas import tpu as pltpu
from jax.sharding import PartitionSpec as P

F32 = jnp.float32
BF16 = jnp.bfloat16
SOFTEN = 0.01
NOW = 11
TICK = 0.0625
GRID = 16.0
LANES = 128
CAP = 64
FINE = 16
VMEM = 44 << 20


def round_bf16(x):
    return x.astype(BF16).astype(F32)


def split2(x):
    a = round_bf16(x)
    return a, round_bf16(x - a)


def split3(x):
    a = round_bf16(x)
    b = round_bf16(x - a)
    return a, b, x - a - b


def coarse(x):
    c = round_bf16(jnp.round(x * GRID) * (1.0 / GRID))
    return c, x - c


def rows_sum(x):
    return jnp.sum(x, axis=0, keepdims=True)


def basis(p, v):
    c, d = coarse(p)
    e, f = coarse(v)
    parts = (c, *split2(d)), (e, *split2(f))
    norms = (
        rows_sum(c * c),
        rows_sum(2.0 * c * d + d * d),
        rows_sum(c * e),
        rows_sum(c * f + d * e + d * f),
    )
    return parts, norms


def select_kernel(
    cnt_hbm, idx_hbm, pos_hbm, vel_hbm, acc_hbm, jerk_hbm, mass_hbm, lev_hbm,
    send_ref, own_ref, pv_ref, idx, cnt, pos, vel, acc, jerk, mass, lev, table, sem,
):
    pairs = (
        (lev_hbm, lev), (pos_hbm, pos), (vel_hbm, vel), (acc_hbm, acc), (jerk_hbm, jerk), (mass_hbm, mass),
        (idx_hbm, idx), (cnt_hbm, cnt),
    )
    copies = [pltpu.make_async_copy(a, b, sem.at[k]) for k, (a, b) in enumerate(pairs)]
    for copy in copies:
        copy.start()
    for copy in copies:
        copy.wait()
    level = lev[...]
    e = (NOW & (jnp.left_shift(jnp.ones_like(level), 4 - level) - 1)).astype(F32) * TICK
    x, u, a, j = pos[...], vel[...], acc[...], jerk[...]
    p = x + e * (u + e * (a * 0.5 + e * j / 6.0))
    v = u + e * (a + e * j * 0.5)
    pv_ref[0:3, :] = p
    pv_ref[3:6, :] = v
    pv_ref[6:7, :] = mass[...]
    table[0:3, :] = p
    table[3:6, :] = v
    table[6:9, :] = a
    table[9:12, :] = j
    table[12:13, :] = e
    slots = jnp.concatenate([idx[0], jnp.zeros((1, LANES - CAP), jnp.int32)], axis=1)
    slots = jnp.broadcast_to(slots, (8, LANES))
    place, owner = slots & (LANES - 1), slots >> 7
    got = [jnp.zeros((8, LANES), F32)] * 2
    for c in range(table.shape[1] // LANES):
        for h in range(2):
            block = table[8 * h : 8 * h + 8, c * LANES : (c + 1) * LANES]
            got[h] = jnp.where(owner == c, jnp.take_along_axis(block, place, axis=1, mode="promise_in_bounds"), got[h])
    got = jnp.concatenate(got, axis=0)
    count = cnt[0, 0]
    own_ref[0:13, :] = got[0:13]
    own_ref[13:16, :] = jnp.full((3, LANES), count.astype(F32))
    row = lax.broadcasted_iota(jnp.int32, (8, LANES), 0)
    live = lax.broadcasted_iota(jnp.int32, (8, LANES), 1) < count
    out = jnp.where(row < 6, jnp.where(live, got[0:8], 0.0), jnp.where(row == 6, count.astype(F32), 0.0))
    for k in range(send_ref.shape[0]):
        send_ref[k] = out


def prepare_kernel(pv_ref, ys_ref, mt_ref, b_ref, m_ref):
    n = pv_ref.shape[1]
    p, v, m = pv_ref[0:3, :], pv_ref[3:6, :], pv_ref[6:7, :]
    (pp, vv), norms = basis(p, v)
    cc, dn, ce, gn = (split3(x) for x in norms)
    ones = jnp.ones((4, n), F32)
    b_ref[0:3, :] = pp[0]
    b_ref[3:6, :] = vv[0]
    for t in range(3):
        b_ref[6 + t : 7 + t, :] = cc[t]
        b_ref[9 + t : 10 + t, :] = ce[t]
    b_ref[12:16, :] = ones
    for k, x in enumerate((*pp, *vv)):
        b_ref[FINE + 3 * k : FINE + 3 * k + 3, :] = x
    b_ref[FINE + 18 : FINE + 20, :] = ones[0:2]
    for t in range(3):
        b_ref[FINE + 20 + t : FINE + 21 + t, :] = dn[t]
        b_ref[FINE + 23 + t : FINE + 24 + t, :] = gn[t]
    b_ref[FINE + 26 : FINE + 32, :] = jnp.zeros((6, n), F32)
    m_ref[...] = jnp.zeros(m_ref.shape, F32)
    for k, x in enumerate((m * p, m * v)):
        for t, y in enumerate(split3(x)):
            m_ref[8 * t + 3 * k : 8 * t + 3 * k + 3, :] = y
    for t, y in enumerate(split3(m)):
        m_ref[8 * t + 6 : 8 * t + 7, :] = y
    mt_ref[...] = m_ref[...].astype(BF16)

    def body(i, _):
        o = pl.multiple_of(i * LANES, LANES)
        x = b_ref[0:FINE, pl.ds(o, LANES)].astype(BF16)
        y = b_ref[FINE : FINE + 32, pl.ds(o, LANES)].astype(BF16)
        ys_ref[pl.ds(o, LANES), :] = jnp.concatenate([x, y, y, y, x], axis=0).T
        return 0

    lax.fori_loop(0, n // LANES, body, 0, unroll=4)


def fill_weights(p, v, wq_ref, wr_ref):
    n = p.shape[1]
    (pp, vv), norms = basis(p, v)
    cc, dn, ce, gn = norms
    cc, dn, ce, gn = split3(cc), split3(dn + SOFTEN), split3(ce), split3(gn)
    wq_ref[...] = jnp.zeros(wq_ref.shape, F32)
    wr_ref[...] = jnp.zeros(wr_ref.shape, F32)
    ones = jnp.ones((3, n), F32)
    wq_ref[0:3, :] = -2.0 * pp[0]
    wr_ref[0:3, :] = -vv[0]
    wr_ref[3:6, :] = -pp[0]
    wq_ref[6:9, :] = ones
    wr_ref[9:12, :] = ones
    for w in range(3):
        wq_ref[12 + w : 13 + w, :] = cc[w]
        wr_ref[12 + w : 13 + w, :] = ce[w]
        o = FINE + 32 * w
        for k in range(3):
            if w or k:
                wq_ref[o + 3 * k : o + 3 * k + 3, :] = -2.0 * pp[w]
                wr_ref[o + 3 * k : o + 3 * k + 3, :] = -vv[w]
                wr_ref[o + 9 + 3 * k : o + 12 + 3 * k, :] = -pp[w]
        wq_ref[o + 18 : o + 19, :] = dn[w]
        wr_ref[o + 18 : o + 19, :] = gn[w]
    wq_ref[FINE + 20 : FINE + 23, :] = ones
    wr_ref[FINE + 23 : FINE + 26, :] = ones


def sweep_kernel(recv_ref, ys_ref, mt_ref, out_ref, act_ref, res_ref, wq_ref, wr_ref, w_ref):
    lists = recv_ref.shape[0]
    stars = ys_ref.shape[0]
    lane = lax.broadcasted_iota(jnp.int32, (8, LANES), 1)
    act_ref[...] = jnp.zeros(act_ref.shape, F32)
    offsets = []
    total = jnp.int32(0)
    chunk = jnp.zeros((8, LANES), F32)
    for k in range(lists):
        offsets.append(total)
        shift = total & (LANES - 1)
        o = pl.multiple_of((total >> 7) * LANES, LANES)
        x = pltpu.roll(recv_ref[k], shift, 1)
        chunk = chunk + jnp.where(lane >= shift, x, 0.0)
        act_ref[:, pl.ds(o, LANES)] = chunk
        total = total + jnp.max(recv_ref[k, 6:7, :].astype(jnp.int32))
        full = (total >> 7) * LANES > o
        chunk = jnp.where(full, jnp.where(lane < shift, x, 0.0), chunk)
    act_ref[:, pl.ds(pl.multiple_of((total >> 7) * LANES, LANES), LANES)] = chunk
    size = wq_ref.shape[1]
    common = size * 5 // 8

    def ready(lo, hi):
        cols = slice(lo, hi)
        fill_weights(act_ref[0:3, cols], act_ref[3:6, cols], wq_ref.at[:, cols], wr_ref.at[:, cols])
        w_ref[0, :, cols] = wq_ref[:, cols].astype(BF16)
        w_ref[1, :, cols] = wr_ref[:, cols].astype(BF16)

    ready(0, common)
    pl.when(total > common)(lambda: ready(common, size))

    def dot(a, b):
        return jnp.dot(a, b, preferred_element_type=F32)

    def strengths(qr):
        q, rw = qr[:, :LANES], qr[:, LANES:]
        inv = lax.rsqrt(q)
        inv2 = inv * inv
        s = inv * inv2
        st = jnp.concatenate([s, s * inv2 * rw], axis=1)
        hi = st.astype(BF16)
        return hi, (st - hi.astype(F32)).astype(BF16)

    def store(cols, s, t):
        p, v = act_ref[0:3, cols], act_ref[3:6, cols]
        res_ref[0:3, cols] = s[0:3] - p * s[6:7]
        res_ref[3:6, cols] = s[3:6] - v * s[6:7] - 3.0 * (t[0:3] - p * t[6:7])

    def tile(t, _):
        cols = pl.ds(pl.multiple_of(t * LANES, LANES), LANES)
        half = stars // 2
        high, low = jnp.zeros((32, 2 * LANES), F32), jnp.zeros((16, 2 * LANES), F32)
        w = jnp.concatenate([w_ref[0, :, cols], w_ref[1, :, cols]], axis=1)
        for h in range(2):
            rows = slice(h * half, (h + 1) * half)
            hi, lo = strengths(dot(ys_ref[rows, :], w))
            high = high + dot(mt_ref[:, rows], hi)
            low = low + dot(mt_ref[0:16, rows], lo)
        x = (high[16:24] + low[8:16]) + (high[8:16] + low[0:8]) + high[0:8]
        store(cols, x[:, :LANES], x[:, LANES:])
        return 0

    def narrow_tile(t, _):
        cols = pl.ds(pl.multiple_of(t * LANES, LANES), LANES)
        half = stars // 2
        first = lax.broadcasted_iota(jnp.int32, (LANES, LANES), 1) < LANES // 2
        weights = []
        for ref in (wq_ref, wr_ref):
            w = jnp.where(first, ref[:, cols], 0.0)
            weights.append(jnp.concatenate([w, pltpu.roll(w, LANES // 2, 1)], axis=0))
        w = jnp.concatenate(weights, axis=1).astype(BF16)
        high, low = jnp.zeros((64, 2 * LANES), F32), jnp.zeros((32, 2 * LANES), F32)
        for h in range(2):
            a = slice(h * half // 2, (h + 1) * half // 2)
            b = slice(half + h * half // 2, half + (h + 1) * half // 2)
            hi, lo = strengths(dot(jnp.concatenate([ys_ref[a, :], ys_ref[b, :]], axis=1), w))
            high = high + dot(jnp.concatenate([mt_ref[:, a], mt_ref[:, b]], axis=0), hi)
            low = low + dot(jnp.concatenate([mt_ref[0:16, a], mt_ref[0:16, b]], axis=0), lo)
        x = (high[16:24] + low[8:16]) + (high[8:16] + low[0:8]) + high[0:8]
        y = (high[48:56] + low[24:32]) + (high[40:48] + low[16:24]) + high[32:40]
        s = x[:, :LANES] + pltpu.roll(y[:, :LANES], LANES // 2, 1)
        t = x[:, LANES:] + pltpu.roll(y[:, LANES:], LANES // 2, 1)
        store(cols, s, t)
        return 0

    rest = total & (LANES - 1)
    whole = (total >> 7) + jnp.where(rest > LANES // 2, 1, 0)
    lax.fori_loop(0, whole, tile, 0)
    lax.fori_loop(whole, (total + (LANES - 1)) >> 7, narrow_tile, 0)
    for k in range(lists):
        shift = offsets[k] & (LANES - 1)
        o = pl.multiple_of((offsets[k] >> 7) * LANES, LANES)
        back = (LANES - shift) & (LANES - 1)
        a = pltpu.roll(res_ref[:, pl.ds(o, LANES)], back, 1)
        b = pltpu.roll(res_ref[:, pl.ds(o + LANES, LANES)], back, 1)
        out_ref[k] = jnp.where(lane < LANES - shift, a, b)


def finish_kernel(recv_ref, own_ref, out_ref):
    x = recv_ref[0]
    for k in range(1, recv_ref.shape[0]):
        x = x + recv_ref[k]
    new_acc, new_jerk = x[0:3, :CAP], x[3:6, :CAP]
    own = own_ref[:, :CAP]
    p, v, acc, jerk, e = own[0:3], own[3:6], own[6:9], own[9:12], own[12:13]
    change = acc - new_acc
    e2 = e * e
    e3 = e2 * e
    e4 = e2 * e2
    snap = (-6.0 * change - e * (4.0 * jerk + 2.0 * new_jerk)) / e2
    crackle = (12.0 * change + 6.0 * e * (jerk + new_jerk)) / e3
    pos = p + e4 / 24.0 * snap + e4 * e / 120.0 * crackle
    vel = v + e3 / 6.0 * snap + e4 / 24.0 * crackle
    live = lax.broadcasted_iota(jnp.int32, (3, CAP), 1).astype(F32) < own[13:14]
    for k, y in enumerate((pos, vel, new_acc, new_jerk)):
        y = jnp.where(live, y, 0.0)
        for c in range(3):
            out_ref[3 * k + c, 0] = y[c : c + 1]


def spec(space):
    return pl.BlockSpec(memory_space=space)


def params(limit=VMEM):
    return pltpu.CompilerParams(vmem_limit_bytes=limit)


def on_device(groups, field_pos, field_vel, field_acc, field_jerk, field_mass, levels, active_index, active_count):
    n = field_pos.shape[1]
    lists = len(groups[0])
    vmem = spec(pltpu.VMEM)
    send, own, pv = pl.pallas_call(
        select_kernel,
        out_shape=(
            jax.ShapeDtypeStruct((lists, 8, LANES), F32),
            jax.ShapeDtypeStruct((16, LANES), F32),
            jax.ShapeDtypeStruct((8, n), F32),
        ),
        in_specs=[spec(pltpu.HBM)] * 8,
        scratch_shapes=[pltpu.VMEM((1, 1, CAP), jnp.int32), pltpu.SMEM((1, 1), jnp.int32)]
        + [pltpu.VMEM((3, n), F32)] * 4
        + [pltpu.VMEM((1, n), F32), pltpu.VMEM((1, n), jnp.int32), pltpu.VMEM((16, n), F32)]
        + [pltpu.SemaphoreType.DMA((8,))],
        compiler_params=params(),
        cost_estimate=pl.CostEstimate(flops=1 << 20, bytes_accessed=1 << 20, transcendentals=0),
        name="select",
    )(active_count, *[
        pltpu.with_memory_space_constraint(x, pltpu.HBM)
        for x in (
            active_index, field_pos, field_vel, field_acc, field_jerk,
            field_mass.reshape(1, n), levels.reshape(1, n),
        )
    ])
    axes = ("blk", "act")
    recv = lax.all_to_all(send, axes, 0, 0, axis_index_groups=groups, tiled=True)
    ys, mt = pl.pallas_call(
        prepare_kernel,
        out_shape=(jax.ShapeDtypeStruct((n, LANES), BF16), jax.ShapeDtypeStruct((32, n), BF16)),
        in_specs=[vmem],
        scratch_shapes=[pltpu.VMEM((FINE + 32, n), F32), pltpu.VMEM((32, n), F32)],
        compiler_params=params(),
        cost_estimate=pl.CostEstimate(flops=1 << 22, bytes_accessed=4 << 20, transcendentals=0),
        name="prepare",
    )(pv)
    size = lists * CAP
    part = pl.pallas_call(
        sweep_kernel,
        out_shape=jax.ShapeDtypeStruct((lists, 8, LANES), F32),
        in_specs=[vmem] * 3,
        scratch_shapes=[pltpu.VMEM((8, size + LANES), F32)] * 2
        + [pltpu.VMEM((LANES, size), F32)] * 2
        + [pltpu.VMEM((2, LANES, size), BF16)],
        compiler_params=params(),
        cost_estimate=pl.CostEstimate(flops=10 << 30, bytes_accessed=4 << 20, transcendentals=0),
        name="sweep",
    )(recv, ys, mt)
    back = lax.all_to_all(part, axes, 0, 0, axis_index_groups=groups, tiled=True)
    out = pl.pallas_call(
        finish_kernel,
        out_shape=jax.ShapeDtypeStruct((12, 1, 1, CAP), F32),
        in_specs=[vmem, vmem],
        compiler_params=params(),
        name="finish",
    )(back, own)
    return out


def list_groups():
    groups = []
    for y in range(4):
        for flip in range(2):
            group = []
            for b in range(16):
                z_hi = (b >> 1) & 1
                z_lo = z_hi ^ flip
                group.append(b * 8 + z_lo * 4 + y)
            groups.append(group)
    return groups


def solution(mesh):
    return jax.shard_map(
        functools.partial(on_device, list_groups()),
        mesh=mesh,
        in_specs=(
            P(None, "blk"),
            P(None, "blk"),
            P(None, "blk"),
            P(None, "blk"),
            P("blk"),
            P("blk"),
            P("blk", "act", None),
            P("blk", "act"),
        ),
        out_specs=P(None, "blk", "act", None),
        check_vma=False,
    )
```

```python
import functools

import jax
import jax.numpy as jnp
from jax import lax
from jax.experimental import pallas as pl
from jax.experimental.pallas import tpu as pltpu
from jax.sharding import PartitionSpec as P

F32 = jnp.float32
BF16 = jnp.bfloat16
SOFTEN = 0.01
NOW = 11
TICK = 0.0625
GRID = 16.0
LANES = 128
CAP = 64
FINE = 16
VMEM = 44 << 20


def round_bf16(x):
    return x.astype(BF16).astype(F32)


def split2(x):
    a = round_bf16(x)
    return a, round_bf16(x - a)


def split3(x):
    a = round_bf16(x)
    b = round_bf16(x - a)
    return a, b, x - a - b


def coarse(x):
    c = round_bf16(jnp.round(x * GRID) * (1.0 / GRID))
    return c, x - c


def rows_sum(x):
    return jnp.sum(x, axis=0, keepdims=True)


def basis(p, v):
    c, d = coarse(p)
    e, f = coarse(v)
    parts = (c, *split2(d)), (e, *split2(f))
    norms = (
        rows_sum(c * c),
        rows_sum(2.0 * c * d + d * d),
        rows_sum(c * e),
        rows_sum(c * f + d * e + d * f),
    )
    return parts, norms


def select_kernel(
    cnt_hbm, idx_hbm, pos_hbm, vel_hbm, acc_hbm, jerk_hbm, mass_hbm, lev_hbm,
    send_ref, own_ref, pv_ref, idx, cnt, pos, vel, acc, jerk, mass, lev, table, sem,
):
    pairs = (
        (lev_hbm, lev), (pos_hbm, pos), (vel_hbm, vel), (acc_hbm, acc), (jerk_hbm, jerk), (mass_hbm, mass),
        (idx_hbm, idx), (cnt_hbm, cnt),
    )
    copies = [pltpu.make_async_copy(a, b, sem.at[k]) for k, (a, b) in enumerate(pairs)]
    for copy in copies:
        copy.start()
    for copy in copies:
        copy.wait()
    level = lev[...]
    e = (NOW & (jnp.left_shift(jnp.ones_like(level), 4 - level) - 1)).astype(F32) * TICK
    x, u, a, j = pos[...], vel[...], acc[...], jerk[...]
    p = x + e * (u + e * (a * 0.5 + e * j / 6.0))
    v = u + e * (a + e * j * 0.5)
    pv_ref[0:3, :] = p
    pv_ref[3:6, :] = v
    pv_ref[6:7, :] = mass[...]
    table[0:3, :] = p
    table[3:6, :] = v
    table[6:9, :] = a
    table[9:12, :] = j
    table[12:13, :] = e
    slots = jnp.concatenate([idx[0], jnp.zeros((1, LANES - CAP), jnp.int32)], axis=1)
    slots = jnp.broadcast_to(slots, (8, LANES))
    place, owner = slots & (LANES - 1), slots >> 7
    got = [jnp.zeros((8, LANES), F32)] * 2
    for c in range(table.shape[1] // LANES):
        for h in range(2):
            block = table[8 * h : 8 * h + 8, c * LANES : (c + 1) * LANES]
            got[h] = jnp.where(owner == c, jnp.take_along_axis(block, place, axis=1, mode="promise_in_bounds"), got[h])
    got = jnp.concatenate(got, axis=0)
    count = cnt[0, 0]
    own_ref[0:13, :] = got[0:13]
    own_ref[13:16, :] = jnp.full((3, LANES), count.astype(F32))
    row = lax.broadcasted_iota(jnp.int32, (8, LANES), 0)
    live = lax.broadcasted_iota(jnp.int32, (8, LANES), 1) < count
    out = jnp.where(row < 6, jnp.where(live, got[0:8], 0.0), jnp.where(row == 6, count.astype(F32), 0.0))
    for k in range(send_ref.shape[0]):
        send_ref[k] = out


def prepare_kernel(pv_ref, ys_ref, mt_ref, b_ref, m_ref):
    n = pv_ref.shape[1]
    p, v, m = pv_ref[0:3, :], pv_ref[3:6, :], pv_ref[6:7, :]
    (pp, vv), norms = basis(p, v)
    cc, dn, ce, gn = (split3(x) for x in norms)
    ones = jnp.ones((4, n), F32)
    b_ref[0:3, :] = pp[0]
    b_ref[3:6, :] = vv[0]
    for t in range(3):
        b_ref[6 + t : 7 + t, :] = cc[t]
        b_ref[9 + t : 10 + t, :] = ce[t]
    b_ref[12:16, :] = ones
    for k, x in enumerate((*pp, *vv)):
        b_ref[FINE + 3 * k : FINE + 3 * k + 3, :] = x
    b_ref[FINE + 18 : FINE + 20, :] = ones[0:2]
    for t in range(3):
        b_ref[FINE + 20 + t : FINE + 21 + t, :] = dn[t]
        b_ref[FINE + 23 + t : FINE + 24 + t, :] = gn[t]
    b_ref[FINE + 26 : FINE + 32, :] = jnp.zeros((6, n), F32)
    m_ref[...] = jnp.zeros(m_ref.shape, F32)
    for k, x in enumerate((m * p, m * v)):
        for t, y in enumerate(split3(x)):
            m_ref[8 * t + 3 * k : 8 * t + 3 * k + 3, :] = y
    for t, y in enumerate(split3(m)):
        m_ref[8 * t + 6 : 8 * t + 7, :] = y
    mt_ref[...] = m_ref[...].astype(BF16)

    def body(i, _):
        o = pl.multiple_of(i * LANES, LANES)
        x = b_ref[0:FINE, pl.ds(o, LANES)].astype(BF16)
        y = b_ref[FINE : FINE + 32, pl.ds(o, LANES)].astype(BF16)
        ys_ref[pl.ds(o, LANES), :] = jnp.concatenate([x, y, y, y, x], axis=0).T
        return 0

    lax.fori_loop(0, n // LANES, body, 0, unroll=4)


def fill_weights(p, v, wq_ref, wr_ref):
    n = p.shape[1]
    (pp, vv), norms = basis(p, v)
    cc, dn, ce, gn = norms
    cc, dn, ce, gn = split3(cc), split3(dn + SOFTEN), split3(ce), split3(gn)
    wq_ref[...] = jnp.zeros(wq_ref.shape, F32)
    wr_ref[...] = jnp.zeros(wr_ref.shape, F32)
    ones = jnp.ones((3, n), F32)
    wq_ref[0:3, :] = -2.0 * pp[0]
    wr_ref[0:3, :] = -vv[0]
    wr_ref[3:6, :] = -pp[0]
    wq_ref[6:9, :] = ones
    wr_ref[9:12, :] = ones
    for w in range(3):
        wq_ref[12 + w : 13 + w, :] = cc[w]
        wr_ref[12 + w : 13 + w, :] = ce[w]
        o = FINE + 32 * w
        for k in range(3):
            if w or k:
                wq_ref[o + 3 * k : o + 3 * k + 3, :] = -2.0 * pp[w]
                wr_ref[o + 3 * k : o + 3 * k + 3, :] = -vv[w]
                wr_ref[o + 9 + 3 * k : o + 12 + 3 * k, :] = -pp[w]
        wq_ref[o + 18 : o + 19, :] = dn[w]
        wr_ref[o + 18 : o + 19, :] = gn[w]
    wq_ref[FINE + 20 : FINE + 23, :] = ones
    wr_ref[FINE + 23 : FINE + 26, :] = ones


def sweep_kernel(recv_ref, ys_ref, mt_ref, out_ref, act_ref, res_ref, wq_ref, wr_ref, w_ref):
    lists = recv_ref.shape[0]
    stars = ys_ref.shape[0]
    lane = lax.broadcasted_iota(jnp.int32, (8, LANES), 1)
    act_ref[...] = jnp.zeros(act_ref.shape, F32)
    offsets = []
    total = jnp.int32(0)
    chunk = jnp.zeros((8, LANES), F32)
    for k in range(lists):
        offsets.append(total)
        shift = total & (LANES - 1)
        o = pl.multiple_of((total >> 7) * LANES, LANES)
        x = pltpu.roll(recv_ref[k], shift, 1)
        chunk = chunk + jnp.where(lane >= shift, x, 0.0)
        act_ref[:, pl.ds(o, LANES)] = chunk
        total = total + jnp.max(recv_ref[k, 6:7, :].astype(jnp.int32))
        full = (total >> 7) * LANES > o
        chunk = jnp.where(full, jnp.where(lane < shift, x, 0.0), chunk)
    act_ref[:, pl.ds(pl.multiple_of((total >> 7) * LANES, LANES), LANES)] = chunk
    size = wq_ref.shape[1]
    common = size * 5 // 8

    def ready(lo, hi):
        cols = slice(lo, hi)
        fill_weights(act_ref[0:3, cols], act_ref[3:6, cols], wq_ref.at[:, cols], wr_ref.at[:, cols])
        w_ref[0, :, cols] = wq_ref[:, cols].astype(BF16)
        w_ref[1, :, cols] = wr_ref[:, cols].astype(BF16)

    ready(0, common)
    pl.when(total > common)(lambda: ready(common, size))

    def dot(a, b):
        return jnp.dot(a, b, preferred_element_type=F32)

    def strengths(qr):
        q, rw = qr[:, :LANES], qr[:, LANES:]
        inv = lax.rsqrt(q)
        inv2 = inv * inv
        s = inv * inv2
        st = jnp.concatenate([s, s * inv2 * rw], axis=1)
        hi = st.astype(BF16)
        return hi, (st - hi.astype(F32)).astype(BF16)

    def store(cols, s, t):
        p, v = act_ref[0:3, cols], act_ref[3:6, cols]
        res_ref[0:3, cols] = s[0:3] - p * s[6:7]
        res_ref[3:6, cols] = s[3:6] - v * s[6:7] - 3.0 * (t[0:3] - p * t[6:7])

    def tile(t, _):
        cols = pl.ds(pl.multiple_of(t * LANES, LANES), LANES)
        half = stars // 2
        high, low = jnp.zeros((32, 2 * LANES), F32), jnp.zeros((16, 2 * LANES), F32)
        w = jnp.concatenate([w_ref[0, :, cols], w_ref[1, :, cols]], axis=1)
        for h in range(2):
            rows = slice(h * half, (h + 1) * half)
            hi, lo = strengths(dot(ys_ref[rows, :], w))
            high = high + dot(mt_ref[:, rows], hi)
            low = low + dot(mt_ref[0:16, rows], lo)
        x = (high[16:24] + low[8:16]) + (high[8:16] + low[0:8]) + high[0:8]
        store(cols, x[:, :LANES], x[:, LANES:])
        return 0

    def narrow_tile(t, _):
        cols = pl.ds(pl.multiple_of(t * LANES, LANES), LANES)
        half = stars // 2
        first = lax.broadcasted_iota(jnp.int32, (LANES, LANES), 1) < LANES // 2
        weights = []
        for ref in (wq_ref, wr_ref):
            w = jnp.where(first, ref[:, cols], 0.0)
            weights.append(jnp.concatenate([w, pltpu.roll(w, LANES // 2, 1)], axis=0))
        w = jnp.concatenate(weights, axis=1).astype(BF16)
        high, low = jnp.zeros((64, 2 * LANES), F32), jnp.zeros((32, 2 * LANES), F32)
        for h in range(2):
            a = slice(h * half // 2, (h + 1) * half // 2)
            b = slice(half + h * half // 2, half + (h + 1) * half // 2)
            hi, lo = strengths(dot(jnp.concatenate([ys_ref[a, :], ys_ref[b, :]], axis=1), w))
            high = high + dot(jnp.concatenate([mt_ref[:, a], mt_ref[:, b]], axis=0), hi)
            low = low + dot(jnp.concatenate([mt_ref[0:16, a], mt_ref[0:16, b]], axis=0), lo)
        x = (high[16:24] + low[8:16]) + (high[8:16] + low[0:8]) + high[0:8]
        y = (high[48:56] + low[24:32]) + (high[40:48] + low[16:24]) + high[32:40]
        s = x[:, :LANES] + pltpu.roll(y[:, :LANES], LANES // 2, 1)
        t = x[:, LANES:] + pltpu.roll(y[:, LANES:], LANES // 2, 1)
        store(cols, s, t)
        return 0

    rest = total & (LANES - 1)
    whole = (total >> 7) + jnp.where(rest > LANES // 2, 1, 0)
    pairs = whole >> 1

    def two_tiles(t, _):
        tile(2 * t, 0)
        return tile(2 * t + 1, 0)

    lax.fori_loop(0, pairs, two_tiles, 0)
    lax.fori_loop(2 * pairs, whole, tile, 0)
    lax.fori_loop(whole, (total + (LANES - 1)) >> 7, narrow_tile, 0)
    for k in range(lists):
        shift = offsets[k] & (LANES - 1)
        o = pl.multiple_of((offsets[k] >> 7) * LANES, LANES)
        back = (LANES - shift) & (LANES - 1)
        a = pltpu.roll(res_ref[:, pl.ds(o, LANES)], back, 1)
        b = pltpu.roll(res_ref[:, pl.ds(o + LANES, LANES)], back, 1)
        out_ref[k] = jnp.where(lane < LANES - shift, a, b)


def finish_kernel(recv_ref, own_ref, out_ref):
    x = recv_ref[0]
    for k in range(1, recv_ref.shape[0]):
        x = x + recv_ref[k]
    new_acc, new_jerk = x[0:3, :CAP], x[3:6, :CAP]
    own = own_ref[:, :CAP]
    p, v, acc, jerk, e = own[0:3], own[3:6], own[6:9], own[9:12], own[12:13]
    change = acc - new_acc
    e2 = e * e
    e3 = e2 * e
    e4 = e2 * e2
    snap = (-6.0 * change - e * (4.0 * jerk + 2.0 * new_jerk)) / e2
    crackle = (12.0 * change + 6.0 * e * (jerk + new_jerk)) / e3
    pos = p + e4 / 24.0 * snap + e4 * e / 120.0 * crackle
    vel = v + e3 / 6.0 * snap + e4 / 24.0 * crackle
    live = lax.broadcasted_iota(jnp.int32, (3, CAP), 1).astype(F32) < own[13:14]
    for k, y in enumerate((pos, vel, new_acc, new_jerk)):
        y = jnp.where(live, y, 0.0)
        for c in range(3):
            out_ref[3 * k + c, 0] = y[c : c + 1]


def spec(space):
    return pl.BlockSpec(memory_space=space)


def params(limit=VMEM):
    return pltpu.CompilerParams(vmem_limit_bytes=limit)


def on_device(groups, field_pos, field_vel, field_acc, field_jerk, field_mass, levels, active_index, active_count):
    n = field_pos.shape[1]
    lists = len(groups[0])
    vmem = spec(pltpu.VMEM)
    send, own, pv = pl.pallas_call(
        select_kernel,
        out_shape=(
            jax.ShapeDtypeStruct((lists, 8, LANES), F32),
            jax.ShapeDtypeStruct((16, LANES), F32),
            jax.ShapeDtypeStruct((8, n), F32),
        ),
        in_specs=[spec(pltpu.HBM)] * 8,
        scratch_shapes=[pltpu.VMEM((1, 1, CAP), jnp.int32), pltpu.SMEM((1, 1), jnp.int32)]
        + [pltpu.VMEM((3, n), F32)] * 4
        + [pltpu.VMEM((1, n), F32), pltpu.VMEM((1, n), jnp.int32), pltpu.VMEM((16, n), F32)]
        + [pltpu.SemaphoreType.DMA((8,))],
        compiler_params=params(),
        cost_estimate=pl.CostEstimate(flops=1 << 20, bytes_accessed=1 << 20, transcendentals=0),
        name="select",
    )(active_count, *[
        pltpu.with_memory_space_constraint(x, pltpu.HBM)
        for x in (
            active_index, field_pos, field_vel, field_acc, field_jerk,
            field_mass.reshape(1, n), levels.reshape(1, n),
        )
    ])
    axes = ("blk", "act")
    recv = lax.all_to_all(send, axes, 0, 0, axis_index_groups=groups, tiled=True)
    ys, mt = pl.pallas_call(
        prepare_kernel,
        out_shape=(jax.ShapeDtypeStruct((n, LANES), BF16), jax.ShapeDtypeStruct((32, n), BF16)),
        in_specs=[vmem],
        scratch_shapes=[pltpu.VMEM((FINE + 32, n), F32), pltpu.VMEM((32, n), F32)],
        compiler_params=params(),
        cost_estimate=pl.CostEstimate(flops=1 << 22, bytes_accessed=4 << 20, transcendentals=0),
        name="prepare",
    )(pv)
    size = lists * CAP
    part = pl.pallas_call(
        sweep_kernel,
        out_shape=jax.ShapeDtypeStruct((lists, 8, LANES), F32),
        in_specs=[vmem] * 3,
        scratch_shapes=[pltpu.VMEM((8, size + LANES), F32)] * 2
        + [pltpu.VMEM((LANES, size), F32)] * 2
        + [pltpu.VMEM((2, LANES, size), BF16)],
        compiler_params=params(),
        cost_estimate=pl.CostEstimate(flops=10 << 30, bytes_accessed=4 << 20, transcendentals=0),
        name="sweep",
    )(recv, ys, mt)
    back = lax.all_to_all(part, axes, 0, 0, axis_index_groups=groups, tiled=True)
    out = pl.pallas_call(
        finish_kernel,
        out_shape=jax.ShapeDtypeStruct((12, 1, 1, CAP), F32),
        in_specs=[vmem, vmem],
        compiler_params=params(),
        name="finish",
    )(back, own)
    return out


def list_groups():
    groups = []
    for y in range(4):
        for flip in range(2):
            group = []
            for b in range(16):
                z_hi = (b >> 1) & 1
                z_lo = z_hi ^ flip
                group.append(b * 8 + z_lo * 4 + y)
            groups.append(group)
    return groups


def solution(mesh):
    return jax.shard_map(
        functools.partial(on_device, list_groups()),
        mesh=mesh,
        in_specs=(
            P(None, "blk"),
            P(None, "blk"),
            P(None, "blk"),
            P(None, "blk"),
            P("blk"),
            P("blk"),
            P("blk", "act", None),
            P("blk", "act"),
        ),
        out_specs=P(None, "blk", "act", None),
        check_vma=False,
    )
```
